768 devices in a mesh: dp: 16 (over y, core), expert: 48 (over x, z).
Axes of the slice: x: 4, y: 8, z: 12, core: 2. Of those that a mesh axis runs over, the one named last changes fastest.
Arguments:
- layer_input: bfloat16 [36864, 2048], P(('dp', 'expert')), may hold values from -60 to 60
- out_grad: bfloat16 [36864, 2048], P(('dp', 'expert')), may hold values from -4 to 4
- router_weight: bfloat16 [96, 2048], replicated, may hold values from -1 to 1
- routes: int32 [36864, 8], P(('dp', 'expert')), may hold values from 0 to 95, all different within a row; in each aligned block of 48 rows (0 to 47, 48 to 95, ...) at most 5 rows name the same one
- hidden_act: bfloat16 [16, 96, 240, 768], P('dp', 'expert'), may hold values from -6 to 6
- down_weight: bfloat16 [96, 768, 2048], P('expert'), may hold values from -0.21875 to 0.21875
Outputs:
- down_grad: float32 [96, 768, 2048], P('expert', None, 'dp')
- hidden_grad: bfloat16 [16, 96, 240, 768], P('dp', 'expert')
- router_grad: float32 [96, 2048], P('expert')
- input_grad: bfloat16 [36864, 2048], P(('dp', 'expert'))
The draws below stay inside these ranges and needn't reach their ends.
Inputs may be any that keep to these rules, and one draw needn't show every extreme that they name: `routes`: each row names 8 different experts; among the rows of one device no expert is named more than 5 times.
All inputs are finite; a program needn't handle non-finite values.
Results may differ from the reference program's by a relative error of at most 0.02.
Values may be sent and summed in bfloat16 or wider, within the bound.
No kernel may reach another device: no remote copies, remote signals or barrier semaphores. Data moves between devices by JAX's collectives and lax.ppermute only.
A program may use at most 128 MiB of HBM per device.

```python
import math
import jax
import jax.numpy as jnp
import numpy as np
from jax import lax

D = 2048
FF = 768
TOP = 8
TOK_DEV = 48
EXPERTS = 96
CAP = 5
SLOTS = 240
TOKENS = 36864
N_DP = 16
N_EXPERT = 48


def draw_router_weight(key, part):
    key = jax.random.fold_in(key, 3)
    fresh_part = jnp.clip(jax.random.normal(key, (EXPERTS, D), jnp.float32), -4.0, 4.0)
    result_rows = fresh_part / jnp.sqrt(1.0 * D)
    return result_rows.astype(jnp.bfloat16)


def draw_layer_input(key, part):
    key = jax.random.fold_in(key, 5)
    key_base = jax.random.fold_in(key, 0)
    base_rows = jnp.clip(jax.random.normal(key_base, (TOKENS, D), jnp.float32), -6.0, 6.0)
    result_rows = base_rows
    return result_rows.astype(jnp.bfloat16)


def block_levels(rng, shape, pieces, low, top_value):
    level, own = 1.0, jax.random.fold_in(rng, 6)
    for dim, parts in pieces:
        heights = jnp.exp(jax.random.uniform(jax.random.fold_in(own, dim), (parts,), jnp.float32, low / len(pieces), top_value / len(pieces)))
        level = level * jnp.repeat(heights, shape[dim] // parts).reshape([-1 if axis == dim else 1 for axis in range(len(shape))])
    return level


def shared_out(own_key, own, number, rows, number_of, top, reach, skew):
    order = jax.random.permutation(own_key, number_of)
    heavy_load, common = portions_of(number_of, rows * top, reach, skew, True), portions_of(number_of, rows * top, reach, skew, False)
    places = jnp.arange(number_of)

    def named(lengths, offset_by):
        used = int((lengths > 0).sum())
        fixed = max(1, used // 4)
        moved = fixed + (places - fixed + offset_by * (used - fixed)) % max(1, number_of - fixed)
        return jnp.zeros((number_of,), jnp.int32).at[order[jnp.where(places < fixed, places, moved)]].set(jnp.asarray(lengths, jnp.int32))

    lengths = jnp.where(number % 4 == 0, named(heavy_load, number // 4), named(common, number - number // 4 - 1))
    mixed = jax.random.permutation(jax.random.fold_in(own, 3), number_of)
    source_of, sink = mixed[0:number_of // 2 * 2:2], mixed[1:number_of // 2 * 2:2]
    room = jnp.minimum(lengths[source_of] - 1, reach - lengths[sink]) // 2
    room = jnp.where((source_of == order[0]) | (sink == order[0]) | (lengths[sink] == 0), 0, jnp.maximum(room, 0))
    moved = jax.random.randint(jax.random.fold_in(own, 4), (number_of // 2,), 0, 1 << 20) % (room + 1)
    lengths = lengths.at[source_of].add(-moved).at[sink].add(moved)
    members = jnp.searchsorted(jnp.cumsum(lengths), jnp.arange(rows * top), side="right").astype(jnp.int32)
    table = members.reshape(top, rows).T
    table = table[jax.random.permutation(jax.random.fold_in(own, 1), rows)]
    offset_by = jax.random.randint(jax.random.fold_in(own, 2), (rows, 1), 0, top)
    return jnp.take_along_axis(table, (jnp.arange(top)[None, :] + offset_by) % top, axis=1)


def portions_of(amount, total, bound, slope, full):
    loads = [(1 << 20) // math.isqrt(standing ** slope) + 1 for standing in range(1, amount + 1)]
    largest = bound if full else min(bound, max(-(-total // amount), total * loads[0] // sum(loads)))
    least = 1 if total - largest >= amount - 1 else 0
    counts, spare = [largest] + [least] * (amount - 1), total - largest - least * (amount - 1)
    while spare > 0:
        free = [i for i in range(1, amount) if counts[i] < largest] or [i for i in range(1, amount) if counts[i] < bound]
        mass, remaining = sum([loads[i] for i in free]), spare
        for i in free:
            more = min(bound - counts[i], max(1, remaining * loads[i] // mass), spare)
            counts[i] = counts[i] + more
            spare = spare - more
    return np.array(counts)


def centred(key, dims, spread, most, pieces=(), held_as=jnp.bfloat16):
    values = spread * jax.random.normal(key, dims, jnp.float32)
    if pieces:
        values = values * block_levels(key, dims, pieces, -0.22, 0.18)
    return jnp.clip(values, -most, most).astype(held_as)


def setup_inputs(seed: int = 0) -> dict:
    keys = jax.random.split(jax.random.key(seed), 7)
    layer_input = draw_layer_input(jax.random.fold_in(keys[6], 71), 0)
    out_grad = centred(keys[1], (TOKENS, D), 0.25, 4.0, ((0, 768),))
    router_weight = draw_router_weight(jax.random.fold_in(keys[6], 71), 0)
    routes_keys = jax.random.split(jax.random.fold_in(keys[3], 1), TOKENS // TOK_DEV)
    routes_turns = jax.random.permutation(jax.random.fold_in(keys[3], 3), TOKENS // TOK_DEV)
    routes = jax.vmap(lambda own, number: shared_out(jax.random.fold_in(keys[3], 2), own, number, TOK_DEV, EXPERTS, TOP, CAP, 2))(routes_keys, routes_turns).reshape((TOKENS, TOP))
    hidden_act = centred(keys[4], (N_DP, EXPERTS, SLOTS, FF), 1.0, 6.0, ((0, 16), (1, 48)))
    down_weight = centred(keys[5], (EXPERTS, FF, D), FF ** -0.5, 0.21875, ((0, 48),))
    return dict(layer_input=layer_input, out_grad=out_grad, router_weight=router_weight, routes=routes, hidden_act=hidden_act, down_weight=down_weight)


def reference(layer_input, out_grad, router_weight, routes, hidden_act, down_weight):
    tokens = layer_input.shape[0]
    experts = router_weight.shape[0]
    blocks = tokens // TOK_DEV
    logits = jnp.einsum("td,ed->te", layer_input.astype(jnp.float32), router_weight.astype(jnp.float32))
    onehot_int = (routes[:, :, None] == jnp.arange(experts, dtype=jnp.int32)).astype(jnp.int32)
    onehot = onehot_int.astype(jnp.float32)
    picked = jnp.sum(onehot * logits[:, None, :], axis=2)
    highest = jnp.max(picked, axis=1, keepdims=True)
    weights = jnp.exp(picked - highest)
    gate_probs = weights / jnp.sum(weights, axis=1, keepdims=True)
    gate_wire = gate_probs.astype(jnp.bfloat16)
    flat_int = onehot_int.reshape(blocks, TOK_DEV * TOP, experts)
    earlier = jnp.cumsum(flat_int, axis=1) - flat_int
    position = jnp.sum(earlier * flat_int, axis=2)
    block_ids = jnp.arange(blocks, dtype=jnp.int32)
    replica_ids = block_ids // N_EXPERT
    source_ids = block_ids % N_EXPERT
    flat_route = routes.reshape(blocks, TOK_DEV * TOP)
    target = (replica_ids[:, None] * experts + flat_route) * SLOTS + source_ids[:, None] * CAP + position
    target = target.reshape(-1).astype(jnp.int32)
    token_ids = jnp.repeat(jnp.arange(tokens, dtype=jnp.int32), TOP)
    slot_token = jnp.full((N_DP * experts * SLOTS,), -1, jnp.int32).at[target].set(token_ids)
    slot_token = slot_token.reshape(N_DP, experts, SLOTS)
    slot_gates = jnp.zeros((N_DP * experts * SLOTS,), jnp.bfloat16).at[target].set(gate_wire.reshape(-1))
    slot_gates = slot_gates.reshape(N_DP, experts, SLOTS)

    def per_expert(expert_id):
        tok_index = slot_token[:, expert_id]
        is_filled = tok_index >= 0
        slot_rows = jnp.where(is_filled[:, :, None], out_grad[jnp.maximum(tok_index, 0)], jnp.zeros((), jnp.bfloat16))
        gate_here = slot_gates[:, expert_id]
        hidden = hidden_act[:, expert_id].astype(jnp.float32)
        weight = down_weight[expert_id].astype(jnp.float32)
        recomputed = jnp.einsum("gsf,fd->gsd", hidden, weight)
        slot_grad = jnp.sum(recomputed * slot_rows.astype(jnp.float32), axis=2)
        scaled = (gate_here.astype(jnp.float32)[:, :, None] * slot_rows.astype(jnp.float32)).astype(jnp.bfloat16)
        grad_here = jnp.einsum("gsd,fd->gsf", scaled.astype(jnp.float32), weight).astype(jnp.bfloat16)
        partial_value = jnp.einsum("gsf,gsd->gfd", hidden, scaled.astype(jnp.float32))
        rounded = lax.optimization_barrier(partial_value.astype(jnp.bfloat16))
        summed = jnp.sum(rounded.astype(jnp.float32), axis=0)
        return summed, grad_here, slot_grad

    down_grad, grad_stack, slot_stack = lax.map(per_expert, jnp.arange(experts, dtype=jnp.int32))
    hidden_grad = jnp.transpose(grad_stack, (1, 0, 2, 3))
    slot_flat = jnp.transpose(slot_stack, (1, 0, 2)).reshape(-1)
    gate_grad = slot_flat[target].reshape(tokens, TOP)
    weighted = jnp.sum(gate_probs * gate_grad, axis=1, keepdims=True)
    picked_grad = gate_probs * (gate_grad - weighted)
    logit_grad = jnp.einsum("tke,tk->te", onehot, picked_grad)
    router_grad = jnp.einsum("te,td->ed", logit_grad, layer_input.astype(jnp.float32), precision=lax.Precision.HIGHEST)
    input_grad = jnp.dot(logit_grad.astype(jnp.bfloat16), router_weight, preferred_element_type=jnp.float32).astype(jnp.bfloat16)
    return down_grad, hidden_grad, router_grad, input_grad
```

```python
import jax
import jax.numpy as jnp
from jax import lax
from jax.sharding import PartitionSpec as P

F32 = jnp.float32
BF16 = jnp.bfloat16


def on_device(layer_input, out_grad, router_weight, routes, hidden_act, down_weight):
    n_expert = lax.axis_size("expert")
    n_dp = lax.axis_size("dp")
    n_y = n_dp // 2
    experts = router_weight.shape[0]
    exp_dev = experts // n_expert
    slots_all = hidden_act.shape[2]
    capacity = slots_all // n_expert
    tok_rows, top_count = routes.shape
    width = out_grad.shape[1]
    send_slots = experts * capacity
    dp_index = lax.axis_index("dp")
    core = dp_index % 2
    y_index = dp_index // 2

    expert_ids = jnp.arange(experts, dtype=jnp.int32)
    chosen = jnp.any(routes[:, :, None] == expert_ids, axis=1)
    logits = jnp.einsum("td,ed->te", layer_input, router_weight, preferred_element_type=F32)
    highest = jnp.max(jnp.where(chosen, logits, -jnp.inf), axis=1, keepdims=True)
    weights = jnp.where(chosen, jnp.exp(jnp.where(chosen, logits - highest, 0.0)), 0.0)
    probs = weights / jnp.sum(weights, axis=1, keepdims=True)
    tok = jnp.arange(tok_rows, dtype=jnp.int32)
    before = (tok[:, None] > tok[None, :]).astype(BF16)
    position = jnp.dot(before, chosen.astype(BF16), preferred_element_type=F32)
    code = jnp.where(chosen, position, -1.0).astype(BF16)
    slot_ids = jnp.arange(send_slots, dtype=jnp.int32)
    spread = (slot_ids[:, None] // capacity == expert_ids[None, :]).astype(BF16)
    code_slot = jnp.einsum("ie,te->it", spread, code, preferred_element_type=F32)
    select = code_slot == (slot_ids % capacity).astype(F32)[:, None]
    select_b = select.astype(BF16)
    send_rows = jnp.dot(select_b, out_grad, preferred_element_type=F32).astype(BF16)
    prob_slot = jnp.einsum("ie,te->it", spread, probs.astype(BF16), preferred_element_type=F32)
    send_gate = jnp.sum(jnp.where(select, prob_slot, 0.0), axis=1).astype(BF16)

    arrived = lax.all_to_all(
        send_rows.reshape(n_expert, exp_dev, capacity, width), "expert", split_axis=0, concat_axis=2, tiled=True
    )[0]
    arrived_gate = lax.all_to_all(
        send_gate.reshape(n_expert, exp_dev, capacity), "expert", split_axis=0, concat_axis=2, tiled=True
    )[0]
    hidden = hidden_act[0]
    gate_wide = arrived_gate.astype(F32)[:, :, None]
    gated_hidden = (gate_wide * hidden.astype(F32)).astype(BF16)

    by_core = arrived.reshape(exp_dev, slots_all, n_y, 2, width // n_dp)
    even, odd = by_core[:, :, :, 0], by_core[:, :, :, 1]
    mine = jnp.where(core == 0, even, odd).reshape(exp_dev, slots_all, width // 2)
    other = jnp.where(core == 0, odd, even).reshape(exp_dev, slots_all, width // 2)
    swap = [(i, i ^ 1) for i in range(n_dp)]
    got_rows = lax.ppermute(other, "dp", swap)
    got_hidden = lax.ppermute(gated_hidden, "dp", swap)

    product = jnp.einsum("esd,efd->esf", arrived, down_weight, preferred_element_type=F32)
    slot_grad = jnp.sum(product * hidden.astype(F32), axis=2)
    hidden_grad = (gate_wide * product).astype(BF16)[None]

    pair_hidden = jnp.concatenate([gated_hidden, got_hidden], axis=1)
    pair_rows = jnp.concatenate([mine, got_rows], axis=1)
    partial_sum = jnp.einsum("esf,esd->efd", pair_hidden, pair_rows, preferred_element_type=F32).astype(BF16)
    blocks = partial_sum.reshape(exp_dev, -1, n_y, width // n_dp).transpose(2, 0, 1, 3)

    def block_at(offset):
        return lax.dynamic_index_in_dim(blocks, (y_index + offset) % n_y, 0, keepdims=False)

    up = [(i, (i + 2) % n_dp) for i in range(n_dp)]
    down = [(i, (i - 2) % n_dp) for i in range(n_dp)]
    half = n_y // 2
    far = block_at(half)
    going_up = lax.ppermute(far[0], "dp", up)
    going_down = lax.ppermute(far[1], "dp", down)
    for step in range(half - 1, 0, -1):
        next_up, next_down = block_at(step), block_at(n_y - step)
        if step == half - 1:
            next_up = jnp.stack([(next_up[0].astype(F32) + going_up.astype(F32)).astype(BF16), next_up[1]])
            next_down = jnp.stack([next_down[0], (next_down[1].astype(F32) + going_down.astype(F32)).astype(BF16)])
        else:
            next_up = (next_up.astype(F32) + going_up.astype(F32)).astype(BF16)
            next_down = (next_down.astype(F32) + going_down.astype(F32)).astype(BF16)
        going_up = lax.ppermute(next_up, "dp", up)
        going_down = lax.ppermute(next_down, "dp", down)
    if half == 1:
        down_grad = block_at(0).astype(F32) + jnp.stack([going_up, going_down]).astype(F32)
    else:
        down_grad = block_at(0).astype(F32) + going_up.astype(F32) + going_down.astype(F32)

    returned = lax.all_to_all(
        slot_grad.reshape(1, exp_dev, n_expert, capacity), "expert", split_axis=2, concat_axis=0, tiled=True
    ).reshape(-1)
    placed = jnp.where(select, returned[:, None], 0.0)
    gate_grad = jnp.einsum("it,ie->te", placed, spread.astype(F32), precision=lax.Precision.HIGHEST)
    weighted = jnp.sum(probs * gate_grad, axis=1, keepdims=True)
    logit_grad = probs * (gate_grad - weighted)
    input_grad = jnp.dot(logit_grad.astype(BF16), router_weight, preferred_element_type=F32).astype(BF16)
    router_term = jnp.einsum(
        "te,td->ed", logit_grad, layer_input.astype(F32), precision=lax.Precision.HIGHEST
    ).astype(BF16)
    shares = lax.all_to_all(
        router_term.reshape(n_expert, exp_dev, width), "expert", split_axis=0, concat_axis=0, tiled=True
    )
    replica_sum = jnp.sum(shares.astype(F32), axis=0)
    copies = jnp.broadcast_to(replica_sum[None], (n_dp, exp_dev, width))
    gathered = lax.all_to_all(copies, "dp", split_axis=0, concat_axis=0, tiled=True)
    router_grad = jnp.sum(gathered, axis=0)
    return (down_grad, hidden_grad, router_grad, input_grad)


def solution(mesh):
    in_specs = (
        P(("dp", "expert"), None),
        P(("dp", "expert"), None),
        P(),
        P(("dp", "expert"), None),
        P("dp", "expert", None, None),
        P("expert", None, None),
    )
    out_specs = (
        P("expert", None, "dp"),
        P("dp", "expert", None, None),
        P("expert", None),
        P(("dp", "expert"), None),
    )
    return jax.shard_map(
        on_device, mesh=mesh, in_specs=in_specs, out_specs=out_specs, check_vma=False
    )
```

```python
import functools

import jax
import jax.numpy as jnp
import numpy as np
from jax import lax
from jax.experimental import pallas as pl
from jax.experimental.pallas import tpu as pltpu
from jax.sharding import PartitionSpec as P

F32 = jnp.float32
BF16 = jnp.bfloat16
LANES = 128
N_X = 4
VMEM_BYTES = 40 * 1024 * 1024


def dot(a, b, dims=((1,), (0,))):
    return lax.dot_general(a, b, (dims, ((), ())), preferred_element_type=F32)


def iota(shape, axis):
    return lax.broadcasted_iota(jnp.int32, shape, axis)


def call(body, out_shape, flops, moved, n_smem=0, **kwargs):
    return pl.pallas_call(
        body,
        out_shape=out_shape,
        compiler_params=pltpu.CompilerParams(vmem_limit_bytes=VMEM_BYTES),
        cost_estimate=pl.CostEstimate(flops=flops, bytes_accessed=moved, transcendentals=0),
        **kwargs,
    )


def whole(n):
    return [pl.BlockSpec(memory_space=pltpu.VMEM)] * n


def route_kernel(x_ref, grad_ref, rw_ref, routes_ref, payload_ref, probs_ref, code_ref):
    experts, width = rw_ref.shape
    top, rows = routes_ref.shape
    ids = iota((experts, rows), 0)
    chosen = ids == routes_ref[0:1, :]
    for k in range(1, top):
        chosen = chosen | (ids == routes_ref[k : k + 1, :])
    logits = dot(rw_ref[...], x_ref[...], ((1,), (1,)))
    highest = jnp.max(jnp.where(chosen, logits, -jnp.inf), axis=0, keepdims=True)
    weights = jnp.where(chosen, jnp.exp(jnp.where(chosen, logits - highest, 0.0)), 0.0)
    probs = weights / jnp.sum(weights, axis=0, keepdims=True)
    earlier = jnp.where(iota((rows, rows), 0) < iota((rows, rows), 1), 1.0, 0.0).astype(BF16)
    position = dot(jnp.where(chosen, 1.0, 0.0).astype(BF16), earlier)
    probs_ref[...] = probs
    code_ref[...] = jnp.where(chosen, position, -1.0)
    marked = jnp.where(chosen, probs, -1.0).astype(BF16)
    turn = jnp.where(iota((experts, LANES), 0) == iota((experts, LANES), 1), 1.0, 0.0).astype(BF16)
    payload_ref[:, :width] = grad_ref[...]
    payload_ref[:, width:] = dot(marked, turn, ((0,), (0,))).astype(BF16)


def pick_kernel(n_blocks, n_z, exp_dev, place_ref, plan_ref, *refs):
    blocks, outs, joined = refs[:n_blocks], refs[n_blocks : n_blocks + N_X], refs[n_blocks + N_X]
    rows, wide = blocks[0].shape
    width = wide - LANES
    total = n_blocks * rows
    for i, block in enumerate(blocks):
        joined[i * rows : (i + 1) * rows, :] = block[...]
    picks = plan_ref.shape[0]
    out_rows = picks // N_X
    shift, local, slot, source = (plan_ref[:, i : i + 1] for i in range(4))
    expert = (((place_ref[0] + shift) & (N_X - 1)) * n_z + place_ref[1]) * exp_dev + local
    wanted = jnp.where(iota((picks, LANES), 1) == expert, 1.0, 0.0).astype(BF16)
    value = dot(wanted, joined[:, width:], ((1,), (1,)))
    here = iota((picks, total), 1)
    base = source * rows
    own = (here >= base) & (here < base + rows)
    chosen = own & (value >= 0.0)
    earlier = jnp.where(iota((total, total), 0) < iota((total, total), 1), 1.0, 0.0).astype(BF16)
    position = dot(jnp.where(chosen, 1.0, 0.0).astype(BF16), earlier)
    picked = chosen & (position == slot.astype(F32))
    gate = jnp.sum(jnp.where(picked, value, 0.0), axis=1, keepdims=True)
    picker = jnp.where(picked, 1.0, 0.0).astype(BF16)
    result = dot(picker, joined[:, :width]).astype(BF16)
    tail = jnp.where(iota((picks, LANES), 1) == 0, gate, 0.0).astype(BF16)
    for i, out in enumerate(outs):
        out[:, :width] = result[i * out_rows : (i + 1) * out_rows]
        out[:, width:] = tail[i * out_rows : (i + 1) * out_rows]


def place_kernel(n_parts, place_ref, target_ref, hidden_ref, *refs):
    parts = refs[:n_parts]
    rows_ref, gate_ref, keep_ref, trade_ref, joined = refs[n_parts:]
    slots, width = rows_ref.shape
    at = 0
    for part in parts:
        joined[at : at + part.shape[0], :] = part[...]
        at += part.shape[0]
    placer = jnp.where(iota((slots, at), 0) == target_ref[...], 1.0, 0.0).astype(BF16)
    gate = dot(placer, joined[:, width:])[:, 0:1]
    gate_ref[...] = gate
    rows_ref[...] = dot(placer, joined[:, :width]).astype(BF16)
    gated = (gate * hidden_ref[...].astype(F32)).astype(BF16)
    n_y = width // (2 * LANES)
    keep_ref[:, width // 2 :] = gated
    trade_ref[:, width // 2 :] = gated
    for k in range(n_y):
        chip = lax.rem(place_ref[2] + k, n_y)
        mine = pl.multiple_of((2 * chip + place_ref[3]) * LANES, LANES)
        other = pl.multiple_of((2 * chip + 1 - place_ref[3]) * LANES, LANES)
        keep_ref[:, k * LANES : (k + 1) * LANES] = rows_ref[:, pl.ds(mine, LANES)]
        trade_ref[:, k * LANES : (k + 1) * LANES] = rows_ref[:, pl.ds(other, LANES)]


def product_kernel(capacity, rows_ref, gate_ref, hidden_ref, weight_ref, grad_ref, back_ref, sums):
    e, f = pl.program_id(0), pl.program_id(1)
    slots = rows_ref.shape[0]
    product = dot(rows_ref[...], weight_ref[0], ((1,), (1,)))
    grad_ref[0, 0] = (gate_ref[...] * product).astype(BF16)
    part = jnp.sum(product * hidden_ref[...].astype(F32), axis=1, keepdims=True)

    @pl.when(f == 0)
    def _():
        sums[...] = part

    @pl.when(f > 0)
    def _():
        sums[...] += part

    @pl.when((e == 0) & (f == 0))
    def _():
        back_ref[...] = jnp.zeros_like(back_ref)

    @pl.when(f == pl.num_programs(1) - 1)
    def _():
        lane = iota((slots, LANES), 1)
        slot = iota((slots, LANES), 0)
        spread = jnp.where(lane == e * capacity + lax.rem(slot, capacity), sums[...], 0.0)
        n_source = back_ref.shape[0]
        first = iota((n_source, slots), 0) * capacity
        slot = iota((n_source, slots), 1)
        group = jnp.where((slot >= first) & (slot < first + capacity), 1.0, 0.0).astype(BF16)
        high = spread.astype(BF16)
        rest = spread - high.astype(F32)
        middle = rest.astype(BF16)
        low = (rest - middle.astype(F32)).astype(BF16)
        back_ref[...] += dot(group, high) + dot(group, middle) + dot(group, low)


def partial_kernel(chunks, mine_ref, got_ref, *outs):
    ff = outs[0].shape[-2]
    half_width = mine_ref.shape[1] - ff
    slots = mine_ref.shape[0]
    exp_dev = 2
    per = slots // exp_dev
    low, high = chunks[0] * LANES, (chunks[-1] + 1) * LANES
    for e in range(exp_dev):
        span = pl.ds(e * per, per)
        total = dot(mine_ref[span, half_width:], mine_ref[span, low:high], ((0,), (0,)))
        total += dot(got_ref[span, half_width:], got_ref[span, low:high], ((0,), (0,)))
        total = total.astype(BF16)
        if len(outs) == exp_dev:
            outs[e][...] = total
        else:
            for i in range(len(chunks)):
                outs[0][i, e] = total[:, i * LANES : (i + 1) * LANES]


def add_kernel(side, blocks_ref, arrived_ref, out_ref):
    if side is None:
        out_ref[...] = (blocks_ref[0].astype(F32) + arrived_ref[...].astype(F32)).astype(BF16)
    else:
        out_ref[side] = (blocks_ref[0, side].astype(F32) + arrived_ref[...].astype(F32)).astype(BF16)
        out_ref[1 - side] = blocks_ref[0, 1 - side]


def router_kernel(capacity, exp_dev, back_ref, probs_ref, code_ref, x_ref, rw_ref, term_ref, grad_ref):
    experts, rows = probs_ref.shape
    n_dev = back_ref.shape[0]
    width = rw_ref.shape[1]
    back = back_ref[...]
    ids = iota((experts, n_dev), 0)
    first = iota((experts, n_dev), 1) * exp_dev
    owner = jnp.where((ids >= first) & (ids < first + exp_dev), 1.0, 0.0).astype(BF16)
    high = back.astype(BF16)
    rest = back - high.astype(F32)
    middle = rest.astype(BF16)
    low = (rest - middle.astype(F32)).astype(BF16)
    spread = dot(owner, high) + dot(owner, middle) + dot(owner, low)
    lane = iota((experts, LANES), 1)
    start = lax.rem(iota((experts, LANES), 0), exp_dev) * capacity
    code = code_ref[...]
    probs = probs_ref[...]
    gate_grad = jnp.zeros((experts, rows), F32)
    for c in range(capacity):
        column = jnp.sum(jnp.where(lane == start + c, spread, 0.0), axis=1, keepdims=True)
        gate_grad += jnp.where(code == c, column, 0.0)
    weighted = jnp.sum(probs * gate_grad, axis=0, keepdims=True)
    logit_grad = probs * (gate_grad - weighted)
    high = logit_grad.astype(BF16)
    low = (logit_grad - high.astype(F32)).astype(BF16)
    grad_ref[...] = dot(high, rw_ref[...], ((0,), (0,))).astype(BF16)
    out_rows, piece = term_ref.shape
    split = width // piece
    row = iota((out_rows, experts), 0)
    first = iota((out_rows, experts), 1) * split
    repeat = jnp.where((row >= first) & (row < first + split), 1.0, 0.0).astype(BF16)
    high = dot(repeat, high).astype(BF16)
    low = dot(repeat, low).astype(BF16)
    quarter = lax.rem(iota((out_rows, 1), 0), split)
    total = jnp.zeros((out_rows, piece), F32)
    for q in range(split):
        x = x_ref[:, q * piece : (q + 1) * piece]
        total += jnp.where(quarter == q, dot(high, x) + dot(low, x), 0.0)
    term_ref[...] = total.astype(BF16)


def batches_of(n_z):
    ahead, back = n_z // 2, (n_z - 1) // 2
    steps = [[0]] + [[s, -s] if s <= back else [s] for s in range(1, ahead + 1)]
    if n_z < 8:
        cuts = [len(steps)]
    else:
        cuts = [len(steps) - 4, len(steps) - 2, len(steps)]
    batches, at = [], 0
    for cut in cuts:
        batches.append([d for step in steps[at:cut] for d in step])
        at = cut
    return batches, ahead, back


def on_device(layer_input, out_grad, router_weight, routes, hidden_act, down_weight):
    n_expert = lax.axis_size("expert")
    n_dp = lax.axis_size("dp")
    n_y, n_z = n_dp // 2, n_expert // N_X
    experts, width = router_weight.shape
    exp_dev = experts // n_expert
    per = hidden_act.shape[2]
    slots = exp_dev * per
    ff = hidden_act.shape[3]
    capacity = per // n_expert
    tok_rows, top_count = routes.shape
    wide = width + LANES
    shape = jax.ShapeDtypeStruct
    dp_index, expert_index = lax.axis_index("dp"), lax.axis_index("expert")
    x_index, z_index = expert_index // n_z, expert_index % n_z
    place = jnp.stack([x_index, z_index, dp_index // 2, dp_index % 2]).astype(jnp.int32)
    smem = pl.BlockSpec(memory_space=pltpu.SMEM)

    payload, probs, code = call(
        route_kernel,
        (shape((tok_rows, wide), BF16), shape((experts, tok_rows), F32), shape((experts, tok_rows), F32)),
        2 * tok_rows * experts * width,
        2 * (2 * tok_rows + experts) * width,
    )(layer_input, out_grad, router_weight, routes.T)

    batches, ahead, behind = batches_of(n_z)
    z_of = lambda shift: [(x * n_z + z, x * n_z + (z + shift) % n_z) for x in range(N_X) for z in range(n_z)]
    x_of = lambda shift: [(x * n_z + z, (x + shift) % N_X * n_z + z) for x in range(N_X) for z in range(n_z)]
    held = {0: payload}
    parts, targets = [], []
    done, due, picked = 0, 0, None
    pick_slots = exp_dev * capacity
    for batch in batches:
        last = max(abs(d) for d in batch)
        while done < last:
            done += 1
            if due == done:
                front, rear = held[done - 1], held[1 - done]
                front, rear, first = lax.optimization_barrier((front, rear, picked[0]))
                held[done - 1], held[1 - done], parts[-N_X] = front, rear, first
            held[done] = lax.ppermute(held[done - 1], "expert", z_of(1))
            if done <= behind:
                held[-done] = lax.ppermute(held[-done + 1], "expert", z_of(-1))
        count = len(batch)
        out_rows = -(-count * pick_slots // 16) * 16
        plan = np.full((N_X, out_rows, 4), -1, np.int32)
        target = np.full((N_X, out_rows, 4), -1, np.int32)
        for shift in range(N_X):
            for i, delta in enumerate(batch):
                for local in range(exp_dev):
                    for c in range(capacity):
                        row = i * pick_slots + local * capacity + c
                        plan[shift, row] = (shift, local, c, i)
                        target[shift, row] = (shift, delta, local, c)
        plan = plan.reshape(N_X * out_rows, 4)
        targets.append(target.reshape(N_X * out_rows, 4))
        picked = call(
            functools.partial(pick_kernel, count, n_z, exp_dev),
            [shape((out_rows, wide), BF16)] * N_X,
            2 * N_X * out_rows * count * tok_rows * width,
            2 * (N_X * out_rows + count * tok_rows) * wide,
            in_specs=[smem] + whole(1 + count),
            out_specs=whole(N_X),
            scratch_shapes=[pltpu.VMEM((count * tok_rows, wide), BF16)],
        )(place, jnp.asarray(plan), *[held[d] for d in batch])
        parts.append(picked[0])
        for shift in range(1, N_X):
            parts.append(lax.ppermute(picked[shift], "expert", x_of(shift)))
        due = last + 2

    table = np.concatenate(targets)
    source = ((x_index - table[:, 0]) % N_X) * n_z + (z_index - table[:, 1]) % n_z
    target = jnp.where(table[:, 2] >= 0, table[:, 2] * per + source * capacity + table[:, 3], -1)
    total_rows = table.shape[0]
    hidden = hidden_act.reshape(slots, ff)
    rows, gate, keep, trade = call(
        functools.partial(place_kernel, len(parts)),
        (
            shape((slots, width), BF16),
            shape((slots, 1), F32),
            shape((slots, width // 2 + ff), BF16),
            shape((slots, width // 2 + ff), BF16),
        ),
        2 * slots * total_rows * wide,
        2 * total_rows * wide + 2 * slots * (2 * width + 3 * ff),
        in_specs=[smem] + whole(2 + len(parts)),
        out_specs=whole(4),
        scratch_shapes=[pltpu.VMEM((total_rows, wide), BF16)],
    )(place, target[None, :].astype(jnp.int32), hidden, *parts)

    got = lax.ppermute(trade, "dp", [(i, i ^ 1) for i in range(n_dp)])

    tile = ff // 2 if ff % 256 == 0 else ff
    hidden_grad, back = call(
        functools.partial(product_kernel, capacity),
        (shape((1, exp_dev, per, ff), BF16), shape((n_expert, LANES), F32)),
        2 * slots * ff * width,
        2 * (slots + exp_dev * ff) * width + 4 * slots * ff,
        grid=(exp_dev, ff // tile),
        in_specs=[
            pl.BlockSpec((per, width), lambda e, f: (e, 0)),
            pl.BlockSpec((per, 1), lambda e, f: (e, 0)),
            pl.BlockSpec((per, tile), lambda e, f: (e, f)),
            pl.BlockSpec((1, tile, width), lambda e, f: (e, f, 0)),
        ],
        out_specs=(
            pl.BlockSpec((1, 1, per, tile), lambda e, f: (0, e, 0, f)),
            pl.BlockSpec((n_expert, LANES), lambda e, f: (0, 0)),
        ),
        scratch_shapes=[pltpu.VMEM((per, 1), F32)],
    )(rows, gate, hidden, down_weight)

    got, back = lax.optimization_barrier((got, back))

    back = lax.all_to_all(back.reshape(n_expert, 1, LANES), "expert", split_axis=0, concat_axis=0, tiled=True)
    piece = exp_dev * width // 8
    term, input_grad = call(
        functools.partial(router_kernel, capacity, exp_dev),
        (shape((n_expert * 8, piece), BF16), shape((tok_rows, width), BF16)),
        2 * tok_rows * width * (experts + 2 * n_expert * 8),
        2 * (2 * tok_rows + 2 * experts) * width,
    )(back.reshape(n_expert, LANES), probs, code, layer_input, router_weight)

    half = n_y // 2
    far_up, far_down = call(
        functools.partial(partial_kernel, [half]),
        [shape((ff, LANES), BF16)] * 2,
        4 * slots * ff * LANES,
        4 * slots * (ff + LANES),
        in_specs=whole(2),
        out_specs=whole(2),
    )(keep, got)
    up = [(i, (i + 2) % n_dp) for i in range(n_dp)]
    down = [(i, (i - 2) % n_dp) for i in range(n_dp)]
    going_up = lax.ppermute(far_up, "dp", up)
    going_down = lax.ppermute(far_down, "dp", down)

    def blocks_of(chunks):
        (blocks,) = call(
            functools.partial(partial_kernel, chunks),
            [shape((len(chunks), exp_dev, ff, LANES), BF16)],
            4 * slots * ff * LANES * len(chunks),
            4 * slots * (ff + LANES * len(chunks)),
            in_specs=whole(2),
            out_specs=whole(1),
        )(keep, got)
        return blocks

    def add_block(blocks, index, arrived):
        side = None if arrived.ndim == 3 else int(blocks is rest)
        size = (1, exp_dev, ff, LANES)
        return call(
            functools.partial(add_kernel, side),
            shape(size[1:], BF16),
            2 * exp_dev * ff * LANES,
            6 * exp_dev * ff * LANES,
            grid=(1,),
            in_specs=[pl.BlockSpec(size, lambda i: (index, 0, 0, 0)), pl.BlockSpec(arrived.shape, lambda i: (0,) * arrived.ndim)],
            out_specs=pl.BlockSpec(size[1:], lambda i: (0, 0, 0)),
        )(blocks, arrived)

    if half > 1:
        near, rest = blocks_of(list(range(half))), blocks_of(list(range(half + 1, n_y)))
    else:
        keep_far = jnp.stack([going_up, going_down])
        both = call(
            functools.partial(partial_kernel, [0]),
            [shape((ff, LANES), BF16)] * 2,
            4 * slots * ff * LANES,
            4 * slots * (ff + LANES),
            in_specs=whole(2),
            out_specs=whole(2),
        )(keep, got)
        down_grad = jnp.stack(both).astype(F32) + keep_far.astype(F32)
    for step in range(half - 1, 0, -1):
        going_up = lax.ppermute(add_block(near, step, going_up), "dp", up)
        going_down = lax.ppermute(add_block(rest, half - 1 - step, going_down), "dp", down)
    if half > 1:
        down_grad = near[0].astype(F32) + going_up.astype(F32) + going_down.astype(F32)

    shares = lax.all_to_all(term.reshape(n_expert, 8, piece), "expert", split_axis=0, concat_axis=0, tiled=True)
    replica_sum = jnp.sum(shares.astype(F32), axis=0)
    copies = jnp.broadcast_to(replica_sum[None], (n_dp, 8, piece))
    gathered = lax.all_to_all(copies, "dp", split_axis=0, concat_axis=0, tiled=True)
    router_grad = jnp.sum(gathered, axis=0).reshape(exp_dev, width)
    return (down_grad, hidden_grad, router_grad, input_grad)


def solution(mesh):
    in_specs = (
        P(("dp", "expert"), None),
        P(("dp", "expert"), None),
        P(),
        P(("dp", "expert"), None),
        P("dp", "expert", None, None),
        P("expert", None, None),
    )
    out_specs = (
        P("expert", None, "dp"),
        P("dp", "expert", None, None),
        P("expert", None),
        P(("dp", "expert"), None),
    )
    return jax.shard_map(
        on_device, mesh=mesh, in_specs=in_specs, out_specs=out_specs, check_vma=False
    )
```

```python
import functools

import jax
import jax.numpy as jnp
import numpy as np
from jax import lax
from jax.experimental import pallas as pl
from jax.experimental.pallas import tpu as pltpu
from jax.sharding import PartitionSpec as P

F32 = jnp.float32
BF16 = jnp.bfloat16
LANES = 128
N_X = 4
VMEM_BYTES = 40 * 1024 * 1024


def dot(a, b, dims=((1,), (0,))):
    return lax.dot_general(a, b, (dims, ((), ())), preferred_element_type=F32)


def iota(shape, axis):
    return lax.broadcasted_iota(jnp.int32, shape, axis)


def call(body, out_shape, flops, moved, n_smem=0, **kwargs):
    return pl.pallas_call(
        body,
        out_shape=out_shape,
        compiler_params=pltpu.CompilerParams(vmem_limit_bytes=VMEM_BYTES),
        cost_estimate=pl.CostEstimate(flops=flops, bytes_accessed=moved, transcendentals=0),
        **kwargs,
    )


def whole(n):
    return [pl.BlockSpec(memory_space=pltpu.VMEM)] * n


def route_kernel(x_ref, grad_ref, rw_ref, routes_ref, first_ref, second_ref, probs_ref, code_ref):
    experts, width = rw_ref.shape
    top, rows = routes_ref.shape
    ids = iota((experts, rows), 0)
    chosen = ids == routes_ref[0:1, :]
    for k in range(1, top):
        chosen = chosen | (ids == routes_ref[k : k + 1, :])
    logits = dot(rw_ref[...], x_ref[...], ((1,), (1,)))
    highest = jnp.max(jnp.where(chosen, logits, -jnp.inf), axis=0, keepdims=True)
    weights = jnp.where(chosen, jnp.exp(jnp.where(chosen, logits - highest, 0.0)), 0.0)
    probs = weights / jnp.sum(weights, axis=0, keepdims=True)
    earlier = jnp.where(iota((rows, rows), 0) < iota((rows, rows), 1), 1.0, 0.0).astype(BF16)
    position = dot(jnp.where(chosen, 1.0, 0.0).astype(BF16), earlier)
    probs_ref[...] = probs
    code_ref[...] = jnp.where(chosen, position, -1.0)
    marked = jnp.where(chosen, probs, -1.0).astype(BF16)
    turn = jnp.where(iota((experts, LANES), 0) == iota((experts, LANES), 1), 1.0, 0.0).astype(BF16)
    marks = dot(marked, turn, ((0,), (0,))).astype(BF16)
    half = width // 2
    for i, ref in enumerate((first_ref, second_ref)):
        ref[:, :half] = grad_ref[:, i * half : (i + 1) * half]
        ref[:, half:] = marks


def pick_kernel(n_pairs, rows, n_z, exp_dev, place_ref, plan_ref, *refs):
    outs, joined = refs[2 * n_pairs : 2 * n_pairs + N_X], refs[2 * n_pairs + N_X]
    half = joined.shape[1] - LANES
    total = joined.shape[0]
    picks = plan_ref.shape[0]
    out_rows = picks // N_X
    shift, local, slot, source = (plan_ref[:, i : i + 1] for i in range(4))
    expert = ((place_ref[0] ^ shift) * n_z + place_ref[1]) * exp_dev + local
    wanted = jnp.where(iota((picks, LANES), 1) == expert, 1.0, 0.0).astype(BF16)
    here = iota((picks, total), 1)
    base = source * rows
    own = (here >= base) & (here < base + rows)
    earlier = jnp.where(iota((total, total), 0) < iota((total, total), 1), 1.0, 0.0).astype(BF16)
    for side in range(2):
        for i, pair in enumerate(refs[side * n_pairs : (side + 1) * n_pairs]):
            joined[2 * i * rows : 2 * (i + 1) * rows, :] = pair[...]
        value = dot(wanted, joined[:, half:], ((1,), (1,)))
        chosen = own & (value >= 0.0)
        position = dot(jnp.where(chosen, 1.0, 0.0).astype(BF16), earlier)
        picked = chosen & (position == slot.astype(F32))
        result = dot(jnp.where(picked, 1.0, 0.0).astype(BF16), joined[:, :half]).astype(BF16)
        at = side * (half + LANES)
        for i, out in enumerate(outs):
            out[:, at : at + half] = result[i * out_rows : (i + 1) * out_rows]
        if side == 0:
            gate = jnp.sum(jnp.where(picked, value, 0.0), axis=1, keepdims=True)
            tail = jnp.where(iota((picks, LANES), 1) == 0, gate, 0.0).astype(BF16)
            for i, out in enumerate(outs):
                out[:, half : half + LANES] = tail[i * out_rows : (i + 1) * out_rows]


def place_kernel(n_parts, order, place_ref, target_ref, hidden_ref, *refs):
    parts = refs[:n_parts]
    rows_ref, gate_ref, keep_ref, trade_ref, joined = refs[n_parts:]
    slots, width = rows_ref.shape
    half = width // 2
    at = 0
    for part in parts:
        joined[at : at + part.shape[0], :] = part[...]
        at += part.shape[0]
    ids = iota((slots, at), 0)
    placer = jnp.where(ids == target_ref[0:1, :], 1.0, 0.0).astype(BF16)
    gate = dot(placer, joined[:, half : half + LANES])[:, 0:1]
    gate_ref[...] = gate
    rows_ref[:, :half] = dot(placer, joined[:, :half]).astype(BF16)
    placer = jnp.where(ids == target_ref[1:2, :], 1.0, 0.0).astype(BF16)
    rows_ref[:, half:] = dot(placer, joined[:, half + LANES :]).astype(BF16)
    gated = (gate * hidden_ref[...].astype(F32)).astype(BF16)
    keep_ref[:, half:] = gated
    trade_ref[:, half:] = gated
    n_y = len(order[0])
    per = slots // len(order)
    for e, deltas in enumerate(order):
        for k, delta in enumerate(deltas):
            chip = lax.rem(place_ref[2] + place_ref[4] * delta + n_y, n_y)
            mine = pl.multiple_of((2 * chip + place_ref[3]) * LANES, LANES)
            other = pl.multiple_of((2 * chip + 1 - place_ref[3]) * LANES, LANES)
            span, column = slice(e * per, (e + 1) * per), slice(k * LANES, (k + 1) * LANES)
            keep_ref[span, column] = rows_ref[span, pl.ds(mine, LANES)]
            trade_ref[span, column] = rows_ref[span, pl.ds(other, LANES)]


def product_kernel(capacity, rows_ref, gate_ref, hidden_ref, weight_ref, grad_ref, back_ref, sums):
    e, f = pl.program_id(0), pl.program_id(1)
    slots = rows_ref.shape[0]
    product = dot(rows_ref[...], weight_ref[0], ((1,), (1,)))
    grad_ref[0, 0] = (gate_ref[...] * product).astype(BF16)
    part = jnp.sum(product * hidden_ref[...].astype(F32), axis=1, keepdims=True)

    @pl.when(f == 0)
    def _():
        sums[...] = part

    @pl.when(f > 0)
    def _():
        sums[...] += part

    @pl.when((e == 0) & (f == 0))
    def _():
        back_ref[...] = jnp.zeros_like(back_ref)

    @pl.when(f == pl.num_programs(1) - 1)
    def _():
        lane = iota((slots, LANES), 1)
        slot = iota((slots, LANES), 0)
        spread = jnp.where(lane == e * capacity + lax.rem(slot, capacity), sums[...], 0.0)
        n_source = back_ref.shape[0]
        first = iota((n_source, slots), 0) * capacity
        slot = iota((n_source, slots), 1)
        group = jnp.where((slot >= first) & (slot < first + capacity), 1.0, 0.0).astype(BF16)
        high = spread.astype(BF16)
        rest = spread - high.astype(F32)
        middle = rest.astype(BF16)
        low = (rest - middle.astype(F32)).astype(BF16)
        back_ref[...] += dot(group, high) + dot(group, middle) + dot(group, low)


def partial_kernel(first, exp_dev, mine_ref, got_ref, *outs):
    ff, wide = outs[0].shape
    half = mine_ref.shape[1] - ff
    per = mine_ref.shape[0] // exp_dev
    groups = len(outs) // exp_dev
    for e in range(exp_dev):
        span = slice(e * per, (e + 1) * per)
        mine, got = mine_ref[span, half:], got_ref[span, half:]
        for g in range(groups):
            column = slice((first + g) * wide, (first + g + 1) * wide)
            total = dot(mine, mine_ref[span, column], ((0,), (0,)))
            total += dot(got, got_ref[span, column], ((0,), (0,)))
            outs[g * exp_dev + e][...] = total.astype(BF16)


def router_kernel(capacity, exp_dev, back_ref, probs_ref, code_ref, x_ref, rw_ref, term_ref, grad_ref):
    experts, rows = probs_ref.shape
    n_dev = back_ref.shape[0]
    width = rw_ref.shape[1]
    back = back_ref[...]
    ids = iota((experts, n_dev), 0)
    first = iota((experts, n_dev), 1) * exp_dev
    owner = jnp.where((ids >= first) & (ids < first + exp_dev), 1.0, 0.0).astype(BF16)
    high = back.astype(BF16)
    rest = back - high.astype(F32)
    middle = rest.astype(BF16)
    low = (rest - middle.astype(F32)).astype(BF16)
    spread = dot(owner, high) + dot(owner, middle) + dot(owner, low)
    lane = iota((experts, LANES), 1)
    start = lax.rem(iota((experts, LANES), 0), exp_dev) * capacity
    code = code_ref[...]
    probs = probs_ref[...]
    gate_grad = jnp.zeros((experts, rows), F32)
    for c in range(capacity):
        column = jnp.sum(jnp.where(lane == start + c, spread, 0.0), axis=1, keepdims=True)
        gate_grad += jnp.where(code == c, column, 0.0)
    weighted = jnp.sum(probs * gate_grad, axis=0, keepdims=True)
    logit_grad = probs * (gate_grad - weighted)
    high = logit_grad.astype(BF16)
    low = (logit_grad - high.astype(F32)).astype(BF16)
    grad_ref[...] = dot(high, rw_ref[...], ((0,), (0,))).astype(BF16)
    out_rows, piece = term_ref.shape
    split = width // piece
    row = iota((out_rows, experts), 0)
    first = iota((out_rows, experts), 1) * split
    repeat = jnp.where((row >= first) & (row < first + split), 1.0, 0.0).astype(BF16)
    high = dot(repeat, high).astype(BF16)
    low = dot(repeat, low).astype(BF16)
    quarter = lax.rem(iota((out_rows, 1), 0), split)
    total = jnp.zeros((out_rows, piece), F32)
    for q in range(split):
        x = x_ref[:, q * piece : (q + 1) * piece]
        total += jnp.where(quarter == q, dot(high, x) + dot(low, x), 0.0)
    term_ref[...] = total.astype(BF16)


def exchange_order(n):
    pairs = [[0, 1]]
    for step in range(1, n // 2):
        pairs.append([-step, -step - 1] if step % 2 else [step, step + 1])
    return pairs


def on_device(layer_input, out_grad, router_weight, routes, hidden_act, down_weight):
    n_expert = lax.axis_size("expert")
    n_dp = lax.axis_size("dp")
    n_y, n_z = n_dp // 2, n_expert // N_X
    experts, width = router_weight.shape
    exp_dev = experts // n_expert
    per = hidden_act.shape[2]
    slots = exp_dev * per
    ff = hidden_act.shape[3]
    capacity = per // n_expert
    tok_rows, top_count = routes.shape
    wide = width + LANES
    shape = jax.ShapeDtypeStruct
    dp_index, expert_index = lax.axis_index("dp"), lax.axis_index("expert")
    x_index, z_index = expert_index // n_z, expert_index % n_z
    y_index = dp_index // 2
    z_sign, y_sign = 1 - 2 * (z_index % 2), 1 - 2 * (y_index % 2)
    place = jnp.stack([x_index, z_index, y_index, dp_index % 2, y_sign]).astype(jnp.int32)
    smem = pl.BlockSpec(memory_space=pltpu.SMEM)
    half_wide = width // 2 + LANES

    first, second, probs, code = call(
        route_kernel,
        (
            shape((tok_rows, half_wide), BF16),
            shape((tok_rows, half_wide), BF16),
            shape((experts, tok_rows), F32),
            shape((experts, tok_rows), F32),
        ),
        2 * tok_rows * experts * width,
        2 * (2 * tok_rows + experts) * width,
    )(layer_input, out_grad, router_weight, routes.T)

    def z_swap(odd):
        one_way = [(x * n_z + z, x * n_z + (z + 1) % n_z) for x in range(N_X) for z in range(odd, n_z, 2)]
        return one_way + [(b, a) for a, b in one_way]

    def x_swap(mask):
        return [(x * n_z + z, (x ^ mask) * n_z + z) for x in range(N_X) for z in range(n_z)]

    offsets = exchange_order(n_z)
    steps = len(offsets)
    cut = steps - 2 if steps > 3 else steps
    batches = [range(0, cut), range(cut, steps)] if cut < steps else [range(steps)]
    other_first = lax.ppermute(first, "expert", z_swap(0))
    other_second = lax.ppermute(second, "expert", z_swap(1))
    held = [[jnp.concatenate([first, other_first]), jnp.concatenate([second, other_second])]]
    parts, targets = [], []
    pick_slots = exp_dev * capacity
    picked, due = None, 0
    for batch in batches:
        while len(held) <= batch[-1]:
            step = len(held)
            if due == step:
                tied = lax.optimization_barrier((held[-1][0], held[-1][1], picked[0]))
                held[-1], parts[0] = list(tied[:2]), tied[2]
            held.append(
                [lax.ppermute(held[-1][side], "expert", z_swap((step + side) % 2)) for side in range(2)]
            )
        count = 2 * len(batch)
        out_rows = -(-count * pick_slots // 16) * 16
        plan = np.full((N_X, out_rows, 4), -1, np.int32)
        target = np.full((N_X, out_rows, 4), -1, np.int32)
        for mask in range(N_X):
            for i in range(count):
                for local in range(exp_dev):
                    for c in range(capacity):
                        row = i * pick_slots + local * capacity + c
                        plan[mask, row] = (mask, local, c, i)
                        target[mask, row] = (mask, offsets[batch[i // 2]][i % 2], local, c)
            plan[mask, count * pick_slots :, 0] = mask
        plan = plan.reshape(N_X * out_rows, 4)
        picked = call(
            functools.partial(pick_kernel, len(batch), tok_rows, n_z, exp_dev),
            [shape((out_rows, width + LANES), BF16)] * N_X,
            2 * N_X * out_rows * count * tok_rows * width,
            2 * (N_X * out_rows + count * tok_rows) * width,
            in_specs=[smem] + whole(1 + count),
            out_specs=whole(N_X),
            scratch_shapes=[pltpu.VMEM((count * tok_rows, half_wide), BF16)],
        )(place, jnp.asarray(plan), *[held[b][0] for b in batch], *[held[b][1] for b in batch])
        due = batch[-1] + 2
        order = [0, 1, 3, 2]
        for mask in order:
            parts.append(lax.ppermute(picked[mask], "expert", x_swap(mask)) if mask else picked[0])
        targets.append(target[order].reshape(N_X * out_rows, 4))

    table = np.concatenate(targets)
    base = table[:, 2] * per + table[:, 3]
    from_x = (x_index ^ np.maximum(table[:, 0], 0)) * n_z
    both = [
        jnp.where(table[:, 2] >= 0, base + (from_x + (z_index + sign * z_sign * table[:, 1]) % n_z) * capacity, -1)
        for sign in (1, -1)
    ]
    target = jnp.stack(both).astype(jnp.int32)
    total_rows = table.shape[0]
    hidden = hidden_act.reshape(slots, ff)
    y_pairs = exchange_order(n_y)
    order = [d for pair in reversed(y_pairs) for d in pair]
    rows, gate, keep, trade = call(
        functools.partial(place_kernel, len(parts), [order, [-d for d in order]]),
        (
            shape((slots, width), BF16),
            shape((slots, 1), F32),
            shape((slots, width // 2 + ff), BF16),
            shape((slots, width // 2 + ff), BF16),
        ),
        2 * slots * total_rows * width,
        2 * total_rows * width + 2 * slots * (2 * width + 3 * ff),
        in_specs=[smem] + whole(2 + len(parts)),
        out_specs=whole(4),
        scratch_shapes=[pltpu.VMEM((total_rows, width + LANES), BF16)],
    )(place, target, hidden, *parts)

    got = lax.ppermute(trade, "dp", [(i, i ^ 1) for i in range(n_dp)])

    tile = ff // 2 if ff % 256 == 0 else ff
    hidden_grad, back = call(
        functools.partial(product_kernel, capacity),
        (shape((1, exp_dev, per, ff), BF16), shape((n_expert, LANES), F32)),
        2 * slots * ff * width,
        2 * (slots + exp_dev * ff) * width + 4 * slots * ff,
        grid=(exp_dev, ff // tile),
        in_specs=[
            pl.BlockSpec((per, width), lambda e, f: (e, 0)),
            pl.BlockSpec((per, 1), lambda e, f: (e, 0)),
            pl.BlockSpec((per, tile), lambda e, f: (e, f)),
            pl.BlockSpec((1, tile, width), lambda e, f: (e, f, 0)),
        ],
        out_specs=(
            pl.BlockSpec((1, 1, per, tile), lambda e, f: (0, e, 0, f)),
            pl.BlockSpec((n_expert, LANES), lambda e, f: (0, 0)),
        ),
        scratch_shapes=[pltpu.VMEM((per, 1), F32)],
    )(rows, gate, hidden, down_weight)

    got, back = lax.optimization_barrier((got, back))
    groups = len(y_pairs)

    def partials(at, count):
        return call(
            functools.partial(partial_kernel, at, exp_dev),
            [shape((ff, 2 * LANES), BF16)] * (exp_dev * count),
            8 * slots * ff * LANES * count,
            4 * slots * (ff + 2 * LANES * count),
            in_specs=whole(2),
            out_specs=whole(exp_dev * count),
        )(keep, got)

    def y_swap(odd):
        one_way = [(2 * y + c, (2 * y + 2 + c) % n_dp) for y in range(odd, n_y, 2) for c in range(2)]
        return one_way + [(b, a) for a, b in one_way]

    def add(a, b):
        return (a.astype(F32) + b.astype(F32)).astype(BF16)

    sums = partials(0, 1)
    later = []
    if groups > 1:
        later = partials(1, groups - 1)
        tied = lax.optimization_barrier((back, *later))
        back, later = tied[0], list(tied[1:])
    for step in range(groups, 1, -1):
        came = [lax.ppermute(sums[e], "dp", y_swap((step - 1 + e) % 2)) for e in range(exp_dev)]
        mine, later = later[:exp_dev], later[exp_dev:]
        if step > 2:
            sums = [add(a, b) for a, b in zip(mine, came)]
        else:
            away = [add(a[:, LANES:], b[:, LANES:]) for a, b in zip(mine, came)]
            home = [a[:, :LANES].astype(F32) + b[:, :LANES].astype(F32) for a, b in zip(mine, came)]
    if groups == 1:
        away = [a[:, LANES:] for a in sums]
        home = [a[:, :LANES].astype(F32) for a in sums]
    came = [lax.ppermute(away[e], "dp", y_swap(e % 2)) for e in range(exp_dev)]
    down_grad = jnp.stack([a + b.astype(F32) for a, b in zip(home, came)])

    back = lax.all_to_all(back.reshape(n_expert, 1, LANES), "expert", split_axis=0, concat_axis=0, tiled=True)
    piece = exp_dev * width // 8
    term, input_grad = call(
        functools.partial(router_kernel, capacity, exp_dev),
        (shape((n_expert * 8, piece), BF16), shape((tok_rows, width), BF16)),
        2 * tok_rows * width * (experts + 2 * n_expert * 8),
        2 * (2 * tok_rows + 2 * experts) * width,
    )(back.reshape(n_expert, LANES), probs, code, layer_input, router_weight)

    shares = lax.all_to_all(term.reshape(n_expert, 8, piece), "expert", split_axis=0, concat_axis=0, tiled=True)
    replica_sum = jnp.sum(shares.astype(F32), axis=0)
    copies = jnp.broadcast_to(replica_sum[None], (n_dp, 8, piece))
    gathered = lax.all_to_all(copies, "dp", split_axis=0, concat_axis=0, tiled=True)
    router_grad = jnp.sum(gathered, axis=0).reshape(exp_dev, width)
    return (down_grad, hidden_grad, router_grad, input_grad)


def solution(mesh):
    in_specs = (
        P(("dp", "expert"), None),
        P(("dp", "expert"), None),
        P(),
        P(("dp", "expert"), None),
        P("dp", "expert", None, None),
        P("expert", None, None),
    )
    out_specs = (
        P("expert", None, "dp"),
        P("dp", "expert", None, None),
        P("expert", None),
        P(("dp", "expert"), None),
    )
    return jax.shard_map(
        on_device, mesh=mesh, in_specs=in_specs, out_specs=out_specs, check_vma=False
    )
```

```python
import functools

import jax
import jax.numpy as jnp
from jax import lax
from jax.experimental import pallas as pl
from jax.experimental.pallas import tpu as pltpu
from jax.sharding import PartitionSpec as P

F32 = jnp.float32
BF16 = jnp.bfloat16
LANES = 128
N_X = 4
VMEM_BYTES = 40 * 1024 * 1024


def dot(a, b, dims=((1,), (0,))):
    return lax.dot_general(a, b, (dims, ((), ())), preferred_element_type=F32)


def iota(shape, axis):
    return lax.broadcasted_iota(jnp.int32, shape, axis)


def call(body, out_shape, flops, moved, n_smem=0, **kwargs):
    return pl.pallas_call(
        body,
        out_shape=out_shape,
        compiler_params=pltpu.CompilerParams(vmem_limit_bytes=VMEM_BYTES),
        cost_estimate=pl.CostEstimate(flops=flops, bytes_accessed=moved, transcendentals=0),
        **kwargs,
    )


def whole(n):
    return [pl.BlockSpec(memory_space=pltpu.VMEM)] * n


def route_kernel(x_ref, grad_ref, rw_ref, routes_ref, first_ref, second_ref, probs_ref, code_ref):
    experts, width = rw_ref.shape
    top, rows = routes_ref.shape
    ids = iota((experts, rows), 0)
    chosen = ids == routes_ref[0:1, :]
    for k in range(1, top):
        chosen = chosen | (ids == routes_ref[k : k + 1, :])
    logits = dot(rw_ref[...], x_ref[...], ((1,), (1,)))
    highest = jnp.max(jnp.where(chosen, logits, -jnp.inf), axis=0, keepdims=True)
    weights = jnp.where(chosen, jnp.exp(jnp.where(chosen, logits - highest, 0.0)), 0.0)
    probs = weights / jnp.sum(weights, axis=0, keepdims=True)
    earlier = jnp.where(iota((rows, rows), 0) < iota((rows, rows), 1), 1.0, 0.0).astype(BF16)
    position = dot(jnp.where(chosen, 1.0, 0.0).astype(BF16), earlier)
    probs_ref[...] = probs
    code_ref[...] = jnp.where(chosen, position, -1.0)
    marked = jnp.where(chosen, probs, -1.0).astype(BF16)
    turn = jnp.where(iota((experts, LANES), 0) == iota((experts, LANES), 1), 1.0, 0.0).astype(BF16)
    marks = dot(marked, turn, ((0,), (0,))).astype(BF16)
    half = width // 2
    for i, ref in enumerate((first_ref, second_ref)):
        ref[:, :half] = grad_ref[:, i * half : (i + 1) * half]
        ref[:, half:] = marks


def split_row(row, exp_dev, capacity):
    pick_slots = exp_dev * capacity
    inner = lax.rem(row, pick_slots)
    return lax.div(row, pick_slots), lax.div(inner, capacity), lax.rem(inner, capacity)


def pick_kernel(n_pairs, rows, n_z, exp_dev, capacity, place_ref, *refs):
    outs, joined = refs[2 * n_pairs : 2 * n_pairs + N_X], refs[2 * n_pairs + N_X]
    half = joined.shape[1] - LANES
    total = joined.shape[0]
    out_rows = outs[0].shape[0]
    picks = N_X * out_rows
    index = iota((picks, 1), 0)
    row = lax.rem(index, out_rows)
    source, local, slot = split_row(row, exp_dev, capacity)
    slot = jnp.where(source < 2 * n_pairs, slot, -1)
    expert = ((place_ref[0] ^ lax.div(index, out_rows)) * n_z + place_ref[1]) * exp_dev + local
    wanted = jnp.where(iota((picks, LANES), 1) == expert, 1.0, 0.0).astype(BF16)
    here = iota((picks, total), 1)
    base = source * rows
    own = (here >= base) & (here < base + rows)
    earlier = jnp.where(iota((total, total), 0) < iota((total, total), 1), 1.0, 0.0).astype(BF16)
    for side in range(2):
        for i, pair in enumerate(refs[side * n_pairs : (side + 1) * n_pairs]):
            joined[2 * i * rows : 2 * (i + 1) * rows, :] = pair[...]
        value = dot(wanted, joined[:, half:], ((1,), (1,)))
        chosen = own & (value >= 0.0)
        position = dot(jnp.where(chosen, 1.0, 0.0).astype(BF16), earlier)
        picked = chosen & (position == slot.astype(F32))
        result = dot(jnp.where(picked, 1.0, 0.0).astype(BF16), joined[:, :half]).astype(BF16)
        at = side * (half + LANES)
        for i, out in enumerate(outs):
            out[:, at : at + half] = result[i * out_rows : (i + 1) * out_rows]
        if side == 0:
            gate = jnp.sum(jnp.where(picked, value, 0.0), axis=1, keepdims=True)
            tail = jnp.where(iota((picks, LANES), 1) == 0, gate, 0.0).astype(BF16)
            for i, out in enumerate(outs):
                out[:, half : half + LANES] = tail[i * out_rows : (i + 1) * out_rows]


def place_kernel(n_parts, n_pairs, n_z, capacity, order, place_ref, hidden_ref, *refs):
    parts = refs[:n_parts]
    rows_ref, gate_ref, keep_ref, trade_ref, joined = refs[n_parts:]
    slots, width = rows_ref.shape
    half = width // 2
    at = 0
    for part in parts:
        joined[at : at + part.shape[0], :] = part[...]
        at += part.shape[0]
    exp_dev = len(order)
    per = slots // exp_dev
    index = iota((1, at), 1)
    part = lax.div(index, parts[0].shape[0])
    block, local, slot = split_row(lax.rem(index, parts[0].shape[0]), exp_dev, capacity)
    turn = lax.rem(part, N_X)
    from_x = (place_ref[0] ^ turn ^ lax.div(turn, 2)) * n_z
    pair = lax.div(part, N_X) * n_pairs + lax.div(block, 2)
    delta = (pair + lax.rem(block, 2)) * (1 - 2 * lax.rem(pair, 2)) * place_ref[5]
    base = local * per + slot
    ids = iota((slots, at), 0)

    def placer_of(sign):
        source = from_x + lax.rem(place_ref[1] + sign * delta + 2 * n_z, n_z)
        target = jnp.where(block < 2 * n_pairs, base + source * capacity, -1)
        return jnp.where(ids == target, 1.0, 0.0).astype(BF16)

    placer = placer_of(1)
    gate = dot(placer, joined[:, half : half + LANES])[:, 0:1]
    gate_ref[...] = gate
    rows_ref[:, :half] = dot(placer, joined[:, :half]).astype(BF16)
    placer = placer_of(-1)
    rows_ref[:, half:] = dot(placer, joined[:, half + LANES :]).astype(BF16)
    gated = (gate * hidden_ref[...].astype(F32)).astype(BF16)
    keep_ref[:, half:] = gated
    trade_ref[:, half:] = gated
    n_y = len(order[0])
    for e, deltas in enumerate(order):
        for k, delta in enumerate(deltas):
            chip = lax.rem(place_ref[2] + place_ref[4] * delta + n_y, n_y)
            mine = pl.multiple_of((2 * chip + place_ref[3]) * LANES, LANES)
            other = pl.multiple_of((2 * chip + 1 - place_ref[3]) * LANES, LANES)
            span, column = slice(e * per, (e + 1) * per), slice(k * LANES, (k + 1) * LANES)
            keep_ref[span, column] = rows_ref[span, pl.ds(mine, LANES)]
            trade_ref[span, column] = rows_ref[span, pl.ds(other, LANES)]


def product_kernel(capacity, rows_ref, gate_ref, hidden_ref, weight_ref, grad_ref, back_ref, sums, total):
    e, f = pl.program_id(0), pl.program_id(1)
    slots = rows_ref.shape[0]
    product = dot(rows_ref[...], weight_ref[0], ((1,), (1,)))
    grad_ref[0, 0] = (gate_ref[...] * product).astype(BF16)
    part = jnp.sum(product * hidden_ref[...].astype(F32), axis=1, keepdims=True)

    @pl.when(f == 0)
    def _():
        sums[...] = part

    @pl.when(f > 0)
    def _():
        sums[...] += part

    @pl.when((e == 0) & (f == 0))
    def _():
        total[...] = jnp.zeros_like(total)

    @pl.when(f == pl.num_programs(1) - 1)
    def _():
        lane = iota((slots, LANES), 1)
        slot = iota((slots, LANES), 0)
        spread = jnp.where(lane == e * capacity + lax.rem(slot, capacity), sums[...], 0.0)
        row = iota((total.shape[0], slots), 0)
        source = lax.div(iota((total.shape[0], slots), 1), capacity)
        high = spread.astype(BF16)
        rest = spread - high.astype(F32)
        middle = rest.astype(BF16)
        low = (rest - middle.astype(F32)).astype(BF16)
        for i, piece in enumerate((high, middle, low)):
            group = jnp.where(row == source * 8 + i, 1.0, 0.0).astype(BF16)
            total[...] += dot(group, piece)

    @pl.when((e == pl.num_programs(0) - 1) & (f == pl.num_programs(1) - 1))
    def _():
        back_ref[...] = total[...].astype(BF16)


def partial_kernel(first, exp_dev, mine_ref, got_ref, *outs):
    ff, wide = outs[0].shape
    half = mine_ref.shape[1] - ff
    per = mine_ref.shape[0] // exp_dev
    groups = len(outs) // exp_dev
    for e in range(exp_dev):
        span = slice(e * per, (e + 1) * per)
        mine, got = mine_ref[span, half:], got_ref[span, half:]
        for g in range(groups):
            column = slice((first + g) * wide, (first + g + 1) * wide)
            total = dot(mine, mine_ref[span, column], ((0,), (0,)))
            total += dot(got, got_ref[span, column], ((0,), (0,)))
            outs[g * exp_dev + e][...] = total.astype(BF16)


def router_kernel(capacity, exp_dev, back_ref, probs_ref, code_ref, x_ref, rw_ref, term_ref, grad_ref):
    experts, rows = probs_ref.shape
    parts = back_ref.shape[0]
    width = rw_ref.shape[1]
    ids = lax.div(iota((experts, parts), 0), exp_dev)
    column = iota((experts, parts), 1)
    owner = jnp.where((lax.div(column, 8) == ids) & (lax.rem(column, 8) < 3), 1.0, 0.0).astype(BF16)
    spread = dot(owner, back_ref[...])
    lane = iota((experts, LANES), 1)
    start = lax.rem(iota((experts, LANES), 0), exp_dev) * capacity
    code = code_ref[...]
    probs = probs_ref[...]
    gate_grad = jnp.zeros((experts, rows), F32)
    for c in range(capacity):
        column = jnp.sum(jnp.where(lane == start + c, spread, 0.0), axis=1, keepdims=True)
        gate_grad += jnp.where(code == c, column, 0.0)
    weighted = jnp.sum(probs * gate_grad, axis=0, keepdims=True)
    logit_grad = probs * (gate_grad - weighted)
    high = logit_grad.astype(BF16)
    low = (logit_grad - high.astype(F32)).astype(BF16)
    grad_ref[...] = dot(high, rw_ref[...], ((0,), (0,))).astype(BF16)
    out_rows, piece = term_ref.shape
    split = width // piece
    row = iota((out_rows, experts), 0)
    first = iota((out_rows, experts), 1) * split
    repeat = jnp.where((row >= first) & (row < first + split), 1.0, 0.0).astype(BF16)
    high = dot(repeat, high).astype(BF16)
    low = dot(repeat, low).astype(BF16)
    quarter = lax.rem(iota((out_rows, 1), 0), split)
    total = jnp.zeros((out_rows, piece), F32)
    for q in range(split):
        x = x_ref[:, q * piece : (q + 1) * piece]
        total += jnp.where(quarter == q, dot(high, x) + dot(low, x), 0.0)
    term_ref[...] = total.astype(BF16)


def exchange_order(n):
    pairs = [[0, 1]]
    for step in range(1, n // 2):
        pairs.append([-step, -step - 1] if step % 2 else [step, step + 1])
    return pairs


def on_device(layer_input, out_grad, router_weight, routes, hidden_act, down_weight):
    n_expert = lax.axis_size("expert")
    n_dp = lax.axis_size("dp")
    n_y, n_z = n_dp // 2, n_expert // N_X
    experts, width = router_weight.shape
    exp_dev = experts // n_expert
    per = hidden_act.shape[2]
    slots = exp_dev * per
    ff = hidden_act.shape[3]
    capacity = per // n_expert
    tok_rows, top_count = routes.shape
    wide = width + LANES
    shape = jax.ShapeDtypeStruct
    dp_index, expert_index = lax.axis_index("dp"), lax.axis_index("expert")
    x_index, z_index = expert_index // n_z, expert_index % n_z
    y_index = dp_index // 2
    z_sign, y_sign = 1 - 2 * (z_index % 2), 1 - 2 * (y_index % 2)
    place = jnp.stack([x_index, z_index, y_index, dp_index % 2, y_sign, z_sign]).astype(jnp.int32)
    smem = pl.BlockSpec(memory_space=pltpu.SMEM)
    half_wide = width // 2 + LANES

    first, second, probs, code = call(
        route_kernel,
        (
            shape((tok_rows, half_wide), BF16),
            shape((tok_rows, half_wide), BF16),
            shape((experts, tok_rows), F32),
            shape((experts, tok_rows), F32),
        ),
        2 * tok_rows * experts * width,
        2 * (2 * tok_rows + experts) * width,
    )(layer_input, out_grad, router_weight, routes.T)

    def z_swap(odd):
        one_way = [(x * n_z + z, x * n_z + (z + 1) % n_z) for x in range(N_X) for z in range(odd, n_z, 2)]
        return one_way + [(b, a) for a, b in one_way]

    def x_swap(mask):
        return [(x * n_z + z, (x ^ mask) * n_z + z) for x in range(N_X) for z in range(n_z)]

    offsets = exchange_order(n_z)
    steps = len(offsets)
    batches = [range(i, i + 2) for i in range(0, steps, 2)]
    other_first = lax.ppermute(first, "expert", z_swap(0))
    other_second = lax.ppermute(second, "expert", z_swap(1))
    held = [[jnp.concatenate([first, other_first]), jnp.concatenate([second, other_second])]]
    parts = []
    pick_slots = exp_dev * capacity
    picked, due = None, 0
    for batch in batches:
        while len(held) <= batch[-1]:
            step = len(held)
            tied_parts = []
            if due == step:
                tied_parts.append(len(parts) - N_X)
            if step >= 4 and step % 2 == 0:
                at = (step - 4) // 2 * N_X
                tied_parts += list(range(at + 1, at + N_X))
            if tied_parts:
                tied = lax.optimization_barrier((*held[-1], *[parts[i] for i in tied_parts]))
                held[-1] = list(tied[:2])
                for i, part in zip(tied_parts, tied[2:]):
                    parts[i] = part
            held.append(
                [lax.ppermute(held[-1][side], "expert", z_swap((step + side) % 2)) for side in range(2)]
            )
        count = 2 * len(batch)
        out_rows = -(-count * pick_slots // 16) * 16
        picked = call(
            functools.partial(pick_kernel, len(batch), tok_rows, n_z, exp_dev, capacity),
            [shape((out_rows, width + LANES), BF16)] * N_X,
            2 * N_X * out_rows * count * tok_rows * width,
            2 * (N_X * out_rows + count * tok_rows) * width,
            in_specs=[smem] + whole(count),
            out_specs=whole(N_X),
            scratch_shapes=[pltpu.VMEM((count * tok_rows, half_wide), BF16)],
        )(place, *[held[b][0] for b in batch], *[held[b][1] for b in batch])
        due = batch[-1] + 2
        for mask in (0, 1, 3, 2):
            parts.append(lax.ppermute(picked[mask], "expert", x_swap(mask)) if mask else picked[0])

    total_rows = len(parts) * out_rows
    hidden = hidden_act.reshape(slots, ff)
    y_pairs = exchange_order(n_y)
    order = [d for pair in reversed(y_pairs) for d in pair]
    rows, gate, keep, trade = call(
        functools.partial(place_kernel, len(parts), 2, n_z, capacity, [order, [-d for d in order]]),
        (
            shape((slots, width), BF16),
            shape((slots, 1), F32),
            shape((slots, width // 2 + ff), BF16),
            shape((slots, width // 2 + ff), BF16),
        ),
        2 * slots * total_rows * width,
        2 * total_rows * width + 2 * slots * (2 * width + 3 * ff),
        in_specs=[smem] + whole(1 + len(parts)),
        out_specs=whole(4),
        scratch_shapes=[pltpu.VMEM((total_rows, width + LANES), BF16)],
    )(place, hidden, *parts)

    got = lax.ppermute(trade, "dp", [(i, i ^ 1) for i in range(n_dp)])

    tile = ff // 2 if ff % 256 == 0 else ff
    hidden_grad, back = call(
        functools.partial(product_kernel, capacity),
        (shape((1, exp_dev, per, ff), BF16), shape((n_expert * 8, LANES), BF16)),
        2 * slots * ff * width,
        2 * (slots + exp_dev * ff) * width + 4 * slots * ff,
        grid=(exp_dev, ff // tile),
        in_specs=[
            pl.BlockSpec((per, width), lambda e, f: (e, 0)),
            pl.BlockSpec((per, 1), lambda e, f: (e, 0)),
            pl.BlockSpec((per, tile), lambda e, f: (e, f)),
            pl.BlockSpec((1, tile, width), lambda e, f: (e, f, 0)),
        ],
        out_specs=(
            pl.BlockSpec((1, 1, per, tile), lambda e, f: (0, e, 0, f)),
            pl.BlockSpec((n_expert * 8, LANES), lambda e, f: (0, 0)),
        ),
        scratch_shapes=[pltpu.VMEM((per, 1), F32), pltpu.VMEM((n_expert * 8, LANES), F32)],
    )(rows, gate, hidden, down_weight)

    got, back = lax.optimization_barrier((got, back))
    groups = len(y_pairs)

    def partials(at, count):
        return call(
            functools.partial(partial_kernel, at, exp_dev),
            [shape((ff, 2 * LANES), BF16)] * (exp_dev * count),
            8 * slots * ff * LANES * count,
            4 * slots * (ff + 2 * LANES * count),
            in_specs=whole(2),
            out_specs=whole(exp_dev * count),
        )(keep, got)

    def y_swap(odd):
        one_way = [(2 * y + c, (2 * y + 2 + c) % n_dp) for y in range(odd, n_y, 2) for c in range(2)]
        return one_way + [(b, a) for a, b in one_way]

    def add(a, b):
        return (a.astype(F32) + b.astype(F32)).astype(BF16)

    sums = partials(0, 1)
    later = []
    if groups > 1:
        later = partials(1, groups - 1)
        tied = lax.optimization_barrier((back, *later))
        back, later = tied[0], list(tied[1:])
    for step in range(groups, 1, -1):
        came = [lax.ppermute(sums[e], "dp", y_swap((step - 1 + e) % 2)) for e in range(exp_dev)]
        mine, later = later[:exp_dev], later[exp_dev:]
        if step > 2:
            sums = [add(a, b) for a, b in zip(mine, came)]
        else:
            away = [add(a[:, LANES:], b[:, LANES:]) for a, b in zip(mine, came)]
            home = [a[:, :LANES].astype(F32) + b[:, :LANES].astype(F32) for a, b in zip(mine, came)]
    if groups == 1:
        away = [a[:, LANES:] for a in sums]
        home = [a[:, :LANES].astype(F32) for a in sums]
    came = [lax.ppermute(away[e], "dp", y_swap(e % 2)) for e in range(exp_dev)]
    down_grad = jnp.stack([a + b.astype(F32) for a, b in zip(home, came)])

    back = lax.all_to_all(back.reshape(n_expert, 8, LANES), "expert", split_axis=0, concat_axis=0, tiled=True)
    piece = exp_dev * width // 8
    term, input_grad = call(
        functools.partial(router_kernel, capacity, exp_dev),
        (shape((n_expert * 8, piece), BF16), shape((tok_rows, width), BF16)),
        2 * tok_rows * width * (experts + 2 * n_expert * 8),
        2 * (2 * tok_rows + 2 * experts) * width,
    )(back.reshape(n_expert * 8, LANES), probs, code, layer_input, router_weight)

    shares = lax.all_to_all(term.reshape(n_expert, 8, piece), "expert", split_axis=0, concat_axis=0, tiled=True)
    replica_sum = jnp.sum(shares.astype(F32), axis=0)
    copies = jnp.broadcast_to(replica_sum[None], (n_dp, 8, piece))
    gathered = lax.all_to_all(copies, "dp", split_axis=0, concat_axis=0, tiled=True)
    router_grad = jnp.sum(gathered, axis=0).reshape(exp_dev, width)
    return (down_grad, hidden_grad, router_grad, input_grad)


def solution(mesh):
    in_specs = (
        P(("dp", "expert"), None),
        P(("dp", "expert"), None),
        P(),
        P(("dp", "expert"), None),
        P("dp", "expert", None, None),
        P("expert", None, None),
    )
    out_specs = (
        P("expert", None, "dp"),
        P("dp", "expert", None, None),
        P("expert", None),
        P(("dp", "expert"), None),
    )
    return jax.shard_map(
        on_device, mesh=mesh, in_specs=in_specs, out_specs=out_specs, check_vma=False
    )
```

```python
import functools

import jax
import jax.numpy as jnp
from jax import lax
from jax.experimental import pallas as pl
from jax.experimental.pallas import tpu as pltpu
from jax.sharding import PartitionSpec as P

F32 = jnp.float32
BF16 = jnp.bfloat16
LANES = 128
VMEM_BYTES = 40 * 1024 * 1024


def dot(a, b, dims=((1,), (0,))):
    return lax.dot_general(a, b, (dims, ((), ())), preferred_element_type=F32)


def iota(shape, axis):
    return lax.broadcasted_iota(jnp.int32, shape, axis)


def call(body, out_shape, flops, moved, n_smem=0, **kwargs):
    return pl.pallas_call(
        body,
        out_shape=out_shape,
        compiler_params=pltpu.CompilerParams(vmem_limit_bytes=VMEM_BYTES),
        cost_estimate=pl.CostEstimate(flops=flops, bytes_accessed=moved, transcendentals=0),
        **kwargs,
    )


def whole(n):
    return [pl.BlockSpec(memory_space=pltpu.VMEM)] * n


def narrow(tiles, out_ref):
    for k in range(tiles.shape[0]):
        out_ref[:, k * LANES : (k + 1) * LANES] = tiles[k].astype(BF16)


def pack(e, exp_dev, capacity, code, grad_ref, buffer):
    experts, rows = code.shape
    n_dev = experts // exp_dev
    piece = grad_ref.shape[1] // 8
    owner = jnp.where(iota((n_dev, experts), 1) == iota((n_dev, experts), 0) * exp_dev + e, 1.0, 0.0).astype(BF16)
    own = dot(owner, code.astype(BF16))
    select = [jnp.where(own == c, 1.0, 0.0) for c in range(capacity)]
    picked = dot(jnp.concatenate(select, axis=0).astype(BF16), grad_ref[...])
    tiles = piece // LANES
    for c in range(capacity):
        for p in range(8):
            for j in range(tiles):
                column = p * piece + j * LANES
                buffer.at[c * tiles + j][pl.ds(p, n_dev, stride=8), :] = picked[
                    c * n_dev : (c + 1) * n_dev, column : column + LANES
                ]
    return owner, select


def route_kernel(exp_dev, capacity, x_ref, grad_ref, rw_ref, routes_ref, chunk_ref, probs_ref, code_ref, buffer):
    experts = rw_ref.shape[0]
    top, rows = routes_ref.shape
    ids = iota((experts, rows), 0)
    chosen = ids == routes_ref[0:1, :]
    for k in range(1, top):
        chosen = chosen | (ids == routes_ref[k : k + 1, :])
    logits = dot(rw_ref[...], x_ref[...], ((1,), (1,)))
    highest = jnp.max(jnp.where(chosen, logits, -jnp.inf), axis=0, keepdims=True)
    weights = jnp.where(chosen, jnp.exp(jnp.where(chosen, logits - highest, 0.0)), 0.0)
    probs = weights / jnp.sum(weights, axis=0, keepdims=True)
    earlier = jnp.where(iota((rows, rows), 0) < iota((rows, rows), 1), 1.0, 0.0).astype(BF16)
    position = dot(jnp.where(chosen, 1.0, 0.0).astype(BF16), earlier)
    code = jnp.where(chosen, position, -1.0)
    probs_ref[...] = probs
    code_ref[...] = code
    n_dev = experts // exp_dev
    lane = iota((n_dev, LANES), 1)
    gates = jnp.zeros((n_dev, LANES), F32)
    for e in reversed(range(exp_dev)):
        if e == 0:
            owner, select = pack(0, exp_dev, capacity, code, grad_ref, buffer)
        else:
            owner = jnp.where(iota((n_dev, experts), 1) == iota((n_dev, experts), 0) * exp_dev + e, 1.0, 0.0)
            owner = owner.astype(BF16)
            own = dot(owner, code.astype(BF16))
            select = [jnp.where(own == c, 1.0, 0.0) for c in range(capacity)]
        own_probs = dot(owner, probs.astype(BF16))
        for c in range(capacity):
            gate = jnp.sum(select[c] * own_probs, axis=1, keepdims=True)
            gates = jnp.where(lane == e * capacity + c, gate, gates)
    for p in range(8):
        buffer.at[buffer.shape[0] - 1][pl.ds(p, n_dev, stride=8), :] = gates
    narrow(buffer, chunk_ref)


def pack_kernel(e, exp_dev, capacity, code_ref, grad_ref, chunk_ref, buffer):
    pack(e, exp_dev, capacity, code_ref[...], grad_ref, buffer)
    narrow(buffer, chunk_ref)


def place_kernel(e, capacity, order, place_ref, hidden_ref, *refs):
    chunk_ref, gates_ref = refs[0], refs[e]
    rows_ref, gate_ref, keep_ref, trade_ref, buffer, wide = refs[1 + e :]
    slots, width = rows_ref.shape
    n_source = slots // capacity
    piece, half = width // 8, width // 2
    tiles = piece // LANES
    for k in range(capacity * tiles):
        buffer[k] = chunk_ref[:, k * LANES : (k + 1) * LANES].astype(F32)
    for c in range(capacity):
        for p in range(8):
            for j in range(tiles):
                wide.at[p * tiles + j][pl.ds(c, n_source, stride=capacity), :] = buffer.at[c * tiles + j][
                    pl.ds(p, n_source, stride=8), :
                ]
    narrow(wide, rows_ref)
    spread = jnp.where(
        iota((slots, n_source * 8), 1) == lax.div(iota((slots, n_source * 8), 0), capacity) * 8, 1.0, 0.0
    ).astype(BF16)
    gates = dot(spread, gates_ref[:, gates_ref.shape[1] - LANES :])
    lane = e * capacity + lax.rem(iota((slots, LANES), 0), capacity)
    gate = jnp.sum(jnp.where(iota((slots, LANES), 1) == lane, gates, 0.0), axis=1, keepdims=True)
    gate_ref[...] = gate
    gated = (gate * hidden_ref[...].astype(F32)).astype(BF16)
    keep_ref[:, half:] = gated
    trade_ref[:, half:] = gated
    n_y = len(order)
    for k, delta in enumerate(order):
        chip = lax.rem(place_ref[0] + place_ref[2] * delta + n_y, n_y)
        mine = pl.multiple_of((2 * chip + place_ref[1]) * LANES, LANES)
        other = pl.multiple_of((2 * chip + 1 - place_ref[1]) * LANES, LANES)
        column = slice(k * LANES, (k + 1) * LANES)
        keep_ref[:, column] = rows_ref[:, pl.ds(mine, LANES)]
        trade_ref[:, column] = rows_ref[:, pl.ds(other, LANES)]


def product_kernel(e, capacity, rows_ref, gate_ref, hidden_ref, weight_ref, *refs):
    if e > 0:
        earlier_ref = refs[0]
        refs = refs[2:]
    grad_ref, back_ref, sums = refs
    f = pl.program_id(0)
    slots = rows_ref.shape[0]
    product = dot(rows_ref[...], weight_ref[0], ((1,), (1,)))
    grad_ref[0, 0] = (gate_ref[...] * product).astype(BF16)
    part = jnp.sum(product * hidden_ref[...].astype(F32), axis=1, keepdims=True)

    @pl.when(f == 0)
    def _():
        sums[...] = part

    @pl.when(f > 0)
    def _():
        sums[...] += part

    @pl.when(f == pl.num_programs(0) - 1)
    def _():
        lane = iota((slots, LANES), 1)
        slot = iota((slots, LANES), 0)
        spread = jnp.where(lane == e * capacity + lax.rem(slot, capacity), sums[...], 0.0)
        row = iota((back_ref.shape[0], slots), 0)
        source = lax.div(iota((back_ref.shape[0], slots), 1), capacity)
        high = spread.astype(BF16)
        rest = spread - high.astype(F32)
        middle = rest.astype(BF16)
        low = (rest - middle.astype(F32)).astype(BF16)
        total = jnp.zeros(back_ref.shape, F32) if e == 0 else earlier_ref[...].astype(F32)
        for i, piece in enumerate((high, middle, low)):
            group = jnp.where(row == source * 8 + i, 1.0, 0.0).astype(BF16)
            total += dot(group, piece)
        back_ref[...] = total.astype(BF16)


def partial_kernel(columns, mine_ref, got_ref, *outs):
    half = mine_ref.shape[1] - outs[0].shape[0] * 2
    for out, (part, blocks) in zip(outs, columns):
        span = slice(half + part * out.shape[0], half + (part + 1) * out.shape[0])
        total = jnp.zeros(out.shape, F32)
        for ref in (mine_ref, got_ref):
            wide = jnp.concatenate([ref[:, b * LANES : (b + 1) * LANES] for b in blocks], axis=1)
            total += dot(ref[:, span], wide, ((0,), (0,)))
        out[...] = total.astype(BF16)


def router_kernel(capacity, exp_dev, back_ref, probs_ref, code_ref, x_ref, rw_ref, term_ref, grad_ref):
    experts, rows = probs_ref.shape
    parts = back_ref.shape[0]
    width = rw_ref.shape[1]
    ids = lax.div(iota((experts, parts), 0), exp_dev)
    column = iota((experts, parts), 1)
    owner = jnp.where((lax.div(column, 8) == ids) & (lax.rem(column, 8) < 3), 1.0, 0.0).astype(BF16)
    spread = dot(owner, back_ref[...])
    lane = iota((experts, LANES), 1)
    start = lax.rem(iota((experts, LANES), 0), exp_dev) * capacity
    code = code_ref[...]
    probs = probs_ref[...]
    gate_grad = jnp.zeros((experts, rows), F32)
    for c in range(capacity):
        column = jnp.sum(jnp.where(lane == start + c, spread, 0.0), axis=1, keepdims=True)
        gate_grad += jnp.where(code == c, column, 0.0)
    weighted = jnp.sum(probs * gate_grad, axis=0, keepdims=True)
    logit_grad = probs * (gate_grad - weighted)
    high = logit_grad.astype(BF16)
    low = (logit_grad - high.astype(F32)).astype(BF16)
    grad_ref[...] = dot(high, rw_ref[...], ((0,), (0,))).astype(BF16)
    out_rows, piece = term_ref.shape
    split = width // piece
    row = iota((out_rows, experts), 0)
    first = iota((out_rows, experts), 1) * split
    repeat = jnp.where((row >= first) & (row < first + split), 1.0, 0.0).astype(BF16)
    high = dot(repeat, high).astype(BF16)
    low = dot(repeat, low).astype(BF16)
    quarter = lax.rem(iota((out_rows, 1), 0), split)
    total = jnp.zeros((out_rows, piece), F32)
    for q in range(split):
        x = x_ref[:, q * piece : (q + 1) * piece]
        total += jnp.where(quarter == q, dot(high, x) + dot(low, x), 0.0)
    term_ref[...] = total.astype(BF16)


def exchange_order(n):
    pairs = [[0, 1]]
    for step in range(1, n // 2):
        pairs.append([-step, -step - 1] if step % 2 else [step, step + 1])
    return pairs


def on_device(layer_input, out_grad, router_weight, routes, hidden_act, down_weight):
    n_expert = lax.axis_size("expert")
    n_dp = lax.axis_size("dp")
    n_y = n_dp // 2
    experts, width = router_weight.shape
    exp_dev = experts // n_expert
    per = hidden_act.shape[2]
    slots = exp_dev * per
    ff = hidden_act.shape[3]
    capacity = per // n_expert
    tok_rows, top_count = routes.shape
    shape = jax.ShapeDtypeStruct
    dp_index, expert_index = lax.axis_index("dp"), lax.axis_index("expert")
    y_index = dp_index // 2
    place = jnp.stack([y_index, dp_index % 2, 1 - 2 * (y_index % 2)]).astype(jnp.int32)
    smem = pl.BlockSpec(memory_space=pltpu.SMEM)
    chunk_rows, chunk_wide = n_expert * 8, capacity * width // 8

    chunk, probs, code = call(
        functools.partial(route_kernel, exp_dev, capacity),
        (
            shape((chunk_rows, chunk_wide + LANES), BF16),
            shape((experts, tok_rows), F32),
            shape((experts, tok_rows), F32),
        ),
        2 * tok_rows * experts * width,
        2 * (2 * tok_rows + experts) * width,
        scratch_shapes=[pltpu.VMEM((chunk_wide // LANES + 1, chunk_rows, LANES), F32)],
    )(layer_input, out_grad, router_weight, routes.T)

    def dispatch(chunk):
        chunk = chunk.reshape(n_expert, 8, chunk.shape[1])
        chunk = lax.all_to_all(chunk, "expert", split_axis=0, concat_axis=0, tiled=True)
        return chunk.reshape(chunk_rows, chunk.shape[2])

    arrived = [dispatch(chunk)]
    for e in range(1, exp_dev):
        chunk = call(
            functools.partial(pack_kernel, e, exp_dev, capacity),
            shape((chunk_rows, chunk_wide), BF16),
            2 * chunk_rows * tok_rows * width,
            2 * chunk_rows * chunk_wide,
            scratch_shapes=[pltpu.VMEM((chunk_wide // LANES, chunk_rows, LANES), F32)],
        )(code, out_grad)
        arrived.append(dispatch(chunk))

    hidden = hidden_act.reshape(slots, ff)
    y_pairs = exchange_order(n_y)
    groups = len(y_pairs)
    order = [d for pair in y_pairs for d in pair]
    block_of = {d % n_y: k for k, d in enumerate(order)}
    tile = ff // 2

    def y_swap(odd):
        one_way = [(2 * y + c, (2 * y + 2 + c) % n_dp) for y in range(odd, n_y, 2) for c in range(2)]
        return one_way + [(b, a) for a, b in one_way]

    def add(a, b):
        return (a.astype(F32) + b.astype(F32)).astype(BF16)

    hidden_grad, back, paced = None, None, None
    down_parts = []
    for e in range(exp_dev):
        if e > 0:
            arrived[e], _ = lax.optimization_barrier((arrived[e], paced))
        inputs = [arrived[e]] + ([arrived[0]] if e else [])
        rows, gate, keep, trade = call(
            functools.partial(place_kernel, e, capacity, order),
            (
                shape((per, width), BF16),
                shape((per, 1), F32),
                shape((per, width // 2 + ff), BF16),
                shape((per, width // 2 + ff), BF16),
            ),
            2 * per * chunk_rows * LANES,
            2 * per * (4 * width + 3 * ff),
            in_specs=[smem, pl.BlockSpec((per, ff), lambda i: (e, 0))] + whole(len(inputs)),
            out_specs=whole(4),
            grid=(1,),
            scratch_shapes=[
                pltpu.VMEM((chunk_wide // LANES, chunk_rows, LANES), F32),
                pltpu.VMEM((width // LANES, per, LANES), F32),
            ],
        )(place, hidden, *inputs)

        got = lax.ppermute(trade, "dp", [(i, i ^ 1) for i in range(n_dp)])

        more, specs, alias = [], [], {}
        if e > 0:
            more = [back, hidden_grad]
            specs = [pl.BlockSpec((chunk_rows, LANES), lambda f: (0, 0)), pl.BlockSpec(memory_space=pl.ANY)]
            alias = {5: 0}
        hidden_grad, back = call(
            functools.partial(product_kernel, e, capacity),
            (shape((1, exp_dev, per, ff), BF16), shape((chunk_rows, LANES), BF16)),
            2 * per * ff * width,
            2 * (per + ff) * width + 4 * per * ff,
            grid=(ff // tile,),
            in_specs=[
                pl.BlockSpec((per, width), lambda f: (0, 0)),
                pl.BlockSpec((per, 1), lambda f: (0, 0)),
                pl.BlockSpec((per, tile), lambda f: (e, f)),
                pl.BlockSpec((1, tile, width), lambda f: (e, f, 0)),
                *specs,
            ],
            out_specs=(
                pl.BlockSpec((1, 1, per, tile), lambda f: (0, e, 0, f)),
                pl.BlockSpec((chunk_rows, LANES), lambda f: (0, 0)),
            ),
            scratch_shapes=[pltpu.VMEM((per, 1), F32)],
            input_output_aliases=alias,
        )(rows, gate, hidden, down_weight, *more)
        got, back = lax.optimization_barrier((got, back))

        def partials(which):
            columns = [
                (half, [block_of[(1 - 2 * half) * d % n_y] for d in y_pairs[g]]) for g in which for half in range(2)
            ]
            return call(
                functools.partial(partial_kernel, columns),
                [shape((tile, 2 * LANES), BF16)] * len(columns),
                4 * per * ff * 2 * LANES * len(which),
                4 * per * (ff + 2 * LANES * len(which)),
                in_specs=whole(2),
                out_specs=whole(len(columns)),
            )(keep, got)

        sums = partials([groups - 1])
        later = list(partials(list(range(groups - 2, -1, -1)))) if groups > 1 else []
        if e == exp_dev - 1:
            back, *later = lax.optimization_barrier((back, *later))
        paced = sums[0]
        for step in range(groups, 1, -1):
            came = [lax.ppermute(sums[h], "dp", y_swap((step - 1 + h) % 2)) for h in range(2)]
            mine, later = later[:2], later[2:]
            if step > 2:
                sums = [add(a, b) for a, b in zip(mine, came)]
                paced = sums[0]
            else:
                away = [add(a[:, LANES:], b[:, LANES:]) for a, b in zip(mine, came)]
                home = [a[:, :LANES].astype(F32) + b[:, :LANES].astype(F32) for a, b in zip(mine, came)]
        if groups == 1:
            away = [a[:, LANES:] for a in sums]
            home = [a[:, :LANES].astype(F32) for a in sums]
        came = [lax.ppermute(away[h], "dp", y_swap(h)) for h in range(2)]
        down_parts += [a + b.astype(F32) for a, b in zip(home, came)]
    down_grad = jnp.concatenate(down_parts).reshape(exp_dev, ff, LANES)

    back = lax.all_to_all(back.reshape(n_expert, 8, LANES), "expert", split_axis=0, concat_axis=0, tiled=True)
    piece = exp_dev * width // 8
    term, input_grad = call(
        functools.partial(router_kernel, capacity, exp_dev),
        (shape((n_expert * 8, piece), BF16), shape((tok_rows, width), BF16)),
        2 * tok_rows * width * (experts + 2 * n_expert * 8),
        2 * (2 * tok_rows + 2 * experts) * width,
    )(back.reshape(n_expert * 8, LANES), probs, code, layer_input, router_weight)

    shares = lax.all_to_all(term.reshape(n_expert, 8, piece), "expert", split_axis=0, concat_axis=0, tiled=True)
    replica_sum = jnp.sum(shares.astype(F32), axis=0)
    copies = jnp.broadcast_to(replica_sum[None], (n_dp, 8, piece))
    gathered = lax.all_to_all(copies, "dp", split_axis=0, concat_axis=0, tiled=True)
    router_grad = jnp.sum(gathered, axis=0).reshape(exp_dev, width)
    return (down_grad, hidden_grad, router_grad, input_grad)


def solution(mesh):
    in_specs = (
        P(("dp", "expert"), None),
        P(("dp", "expert"), None),
        P(),
        P(("dp", "expert"), None),
        P("dp", "expert", None, None),
        P("expert", None, None),
    )
    out_specs = (
        P("expert", None, "dp"),
        P("dp", "expert", None, None),
        P("expert", None),
        P(("dp", "expert"), None),
    )
    return jax.shard_map(
        on_device, mesh=mesh, in_specs=in_specs, out_specs=out_specs, check_vma=False
    )
```

```python
import functools

import jax
import jax.numpy as jnp
from jax import lax
from jax.experimental import pallas as pl
from jax.experimental.pallas import tpu as pltpu
from jax.sharding import PartitionSpec as P

F32 = jnp.float32
BF16 = jnp.bfloat16
LANES = 128
VMEM_BYTES = 28 * 1024 * 1024


def dot(a, b, dims=((1,), (0,))):
    return lax.dot_general(a, b, (dims, ((), ())), preferred_element_type=F32)


def iota(shape, axis):
    return lax.broadcasted_iota(jnp.int32, shape, axis)


def call(body, out_shape, flops, moved, n_smem=0, **kwargs):
    return pl.pallas_call(
        body,
        out_shape=out_shape,
        compiler_params=pltpu.CompilerParams(vmem_limit_bytes=VMEM_BYTES),
        cost_estimate=pl.CostEstimate(flops=flops, bytes_accessed=moved, transcendentals=0),
        **kwargs,
    )


def whole(n):
    return [pl.BlockSpec(memory_space=pltpu.VMEM)] * n


def narrow(tiles, out_ref):
    for k in range(tiles.shape[0]):
        out_ref[:, k * LANES : (k + 1) * LANES] = tiles[k].astype(BF16)


def route_kernel(exp_dev, capacity, x_ref, grad_ref, rw_ref, routes_ref, chunk_ref, probs_ref, code_ref, buffer):
    experts = rw_ref.shape[0]
    top, rows = routes_ref.shape
    ids = iota((experts, rows), 0)
    chosen = ids == routes_ref[0:1, :]
    for k in range(1, top):
        chosen = chosen | (ids == routes_ref[k : k + 1, :])
    logits = dot(rw_ref[...], x_ref[...], ((1,), (1,)))
    highest = jnp.max(jnp.where(chosen, logits, -jnp.inf), axis=0, keepdims=True)
    weights = jnp.where(chosen, jnp.exp(jnp.where(chosen, logits - highest, 0.0)), 0.0)
    probs = weights / jnp.sum(weights, axis=0, keepdims=True)
    earlier = jnp.where(iota((rows, rows), 0) < iota((rows, rows), 1), 1.0, 0.0).astype(BF16)
    position = dot(jnp.where(chosen, 1.0, 0.0).astype(BF16), earlier)
    code = jnp.where(chosen, position, -1.0)
    probs_ref[...] = probs
    code_ref[...] = code
    n_dev = experts // exp_dev
    lane = iota((n_dev, LANES), 1)
    gates = jnp.zeros((n_dev, LANES), F32)
    piece = grad_ref.shape[1] // 8
    tiles = piece // LANES
    for e in range(exp_dev):
        owner = jnp.where(iota((n_dev, experts), 1) == iota((n_dev, experts), 0) * exp_dev + e, 1.0, 0.0).astype(BF16)
        own = dot(owner, code.astype(BF16))
        own_probs = dot(owner, probs.astype(BF16))
        select = [jnp.where(own == c, 1.0, 0.0) for c in range(capacity)]
        picked = dot(jnp.concatenate(select, axis=0).astype(BF16), grad_ref[...])
        for c in range(capacity):
            gate = jnp.sum(select[c] * own_probs, axis=1, keepdims=True)
            gates = jnp.where(lane == e * capacity + c, gate, gates)
            for p in range(8):
                for j in range(tiles):
                    column = p * piece + j * LANES
                    buffer.at[(e * capacity + c) * tiles + j][pl.ds(p, n_dev, stride=8), :] = picked[
                        c * n_dev : (c + 1) * n_dev, column : column + LANES
                    ]
    for p in range(8):
        buffer.at[buffer.shape[0] - 1][pl.ds(p, n_dev, stride=8), :] = gates
    narrow(buffer, chunk_ref)


def place_kernel(capacity, order, place_ref, hidden_ref, chunk_ref, rows_ref, gate_ref, keep_ref, trade_ref, buffer, wide):
    slots, width = rows_ref.shape
    exp_dev = len(order)
    per = slots // exp_dev
    n_source = per // capacity
    piece, half = width // 8, width // 2
    tiles = piece // LANES
    spread = jnp.where(
        iota((per, n_source * 8), 1) == lax.div(iota((per, n_source * 8), 0), capacity) * 8, 1.0, 0.0
    ).astype(BF16)
    gates = dot(spread, chunk_ref[:, chunk_ref.shape[1] - LANES :])
    n_y = len(order[0])
    for e in range(exp_dev):
        span = slice(e * per, (e + 1) * per)
        for k in range(capacity * tiles):
            at = e * capacity * tiles + k
            buffer[k] = chunk_ref[:, at * LANES : (at + 1) * LANES].astype(F32)
        for c in range(capacity):
            for p in range(8):
                for j in range(tiles):
                    wide.at[p * tiles + j][pl.ds(c, n_source, stride=capacity), :] = buffer.at[c * tiles + j][
                        pl.ds(p, n_source, stride=8), :
                    ]
        for k in range(width // LANES):
            rows_ref[span, k * LANES : (k + 1) * LANES] = wide[k].astype(BF16)
        lane = e * capacity + lax.rem(iota((per, LANES), 0), capacity)
        gate = jnp.sum(jnp.where(iota((per, LANES), 1) == lane, gates, 0.0), axis=1, keepdims=True)
        gate_ref[span, :] = gate
        gated = (gate * hidden_ref[span, :].astype(F32)).astype(BF16)
        keep_ref[span, half:] = gated
        trade_ref[span, half:] = gated
        for k, delta in enumerate(order[e]):
            chip = lax.rem(place_ref[0] + place_ref[2] * delta + n_y, n_y)
            mine = pl.multiple_of((2 * chip + place_ref[1]) * LANES, LANES)
            other = pl.multiple_of((2 * chip + 1 - place_ref[1]) * LANES, LANES)
            column = slice(k * LANES, (k + 1) * LANES)
            keep_ref[span, column] = rows_ref[span, pl.ds(mine, LANES)]
            trade_ref[span, column] = rows_ref[span, pl.ds(other, LANES)]


def product_kernel(capacity, rows_ref, gate_ref, hidden_ref, weight_ref, grad_ref, back_ref, sums, total):
    e, f = pl.program_id(0), pl.program_id(1)
    slots = rows_ref.shape[0]
    product = dot(rows_ref[...], weight_ref[0], ((1,), (1,)))
    grad_ref[0, 0] = (gate_ref[...] * product).astype(BF16)
    part = jnp.sum(product * hidden_ref[...].astype(F32), axis=1, keepdims=True)

    @pl.when(f == 0)
    def _():
        sums[...] = part

    @pl.when(f > 0)
    def _():
        sums[...] += part

    @pl.when((e == 0) & (f == 0))
    def _():
        total[...] = jnp.zeros_like(total)

    @pl.when(f == pl.num_programs(1) - 1)
    def _():
        lane = iota((slots, LANES), 1)
        slot = iota((slots, LANES), 0)
        spread = jnp.where(lane == e * capacity + lax.rem(slot, capacity), sums[...], 0.0)
        row = iota((total.shape[0], slots), 0)
        source = lax.div(iota((total.shape[0], slots), 1), capacity)
        high = spread.astype(BF16)
        rest = spread - high.astype(F32)
        middle = rest.astype(BF16)
        low = (rest - middle.astype(F32)).astype(BF16)
        for i, piece in enumerate((high, middle, low)):
            group = jnp.where(row == source * 8 + i, 1.0, 0.0).astype(BF16)
            total[...] += dot(group, piece)

    @pl.when((e == pl.num_programs(0) - 1) & (f == pl.num_programs(1) - 1))
    def _():
        back_ref[...] = total[...].astype(BF16)


def partial_kernel(first, exp_dev, mine_ref, got_ref, *outs):
    ff, wide = outs[0].shape
    half = mine_ref.shape[1] - ff
    per = mine_ref.shape[0] // exp_dev
    groups = len(outs) // exp_dev
    for e in range(exp_dev):
        span = slice(e * per, (e + 1) * per)
        mine, got = mine_ref[span, half:], got_ref[span, half:]
        for g in range(groups):
            column = slice((first + g) * wide, (first + g + 1) * wide)
            total = dot(mine, mine_ref[span, column], ((0,), (0,)))
            total += dot(got, got_ref[span, column], ((0,), (0,)))
            outs[g * exp_dev + e][...] = total.astype(BF16)


def router_kernel(capacity, exp_dev, back_ref, probs_ref, code_ref, x_ref, rw_ref, term_ref, grad_ref):
    experts, rows = probs_ref.shape
    parts = back_ref.shape[0]
    width = rw_ref.shape[1]
    ids = lax.div(iota((experts, parts), 0), exp_dev)
    column = iota((experts, parts), 1)
    owner = jnp.where((lax.div(column, 8) == ids) & (lax.rem(column, 8) < 3), 1.0, 0.0).astype(BF16)
    spread = dot(owner, back_ref[...])
    lane = iota((experts, LANES), 1)
    start = lax.rem(iota((experts, LANES), 0), exp_dev) * capacity
    code = code_ref[...]
    probs = probs_ref[...]
    gate_grad = jnp.zeros((experts, rows), F32)
    for c in range(capacity):
        column = jnp.sum(jnp.where(lane == start + c, spread, 0.0), axis=1, keepdims=True)
        gate_grad += jnp.where(code == c, column, 0.0)
    weighted = jnp.sum(probs * gate_grad, axis=0, keepdims=True)
    logit_grad = probs * (gate_grad - weighted)
    high = logit_grad.astype(BF16)
    low = (logit_grad - high.astype(F32)).astype(BF16)
    grad_ref[...] = dot(high, rw_ref[...], ((0,), (0,))).astype(BF16)
    out_rows, piece = term_ref.shape
    split = width // piece
    row = iota((out_rows, experts), 0)
    first = iota((out_rows, experts), 1) * split
    repeat = jnp.where((row >= first) & (row < first + split), 1.0, 0.0).astype(BF16)
    high = dot(repeat, high).astype(BF16)
    low = dot(repeat, low).astype(BF16)
    quarter = lax.rem(iota((out_rows, 1), 0), split)
    total = jnp.zeros((out_rows, piece), F32)
    for q in range(split):
        x = x_ref[:, q * piece : (q + 1) * piece]
        total += jnp.where(quarter == q, dot(high, x) + dot(low, x), 0.0)
    term_ref[...] = total.astype(BF16)


def exchange_order(n):
    pairs = [[0, 1]]
    for step in range(1, n // 2):
        pairs.append([-step, -step - 1] if step % 2 else [step, step + 1])
    return pairs


def on_device(layer_input, out_grad, router_weight, routes, hidden_act, down_weight):
    n_expert = lax.axis_size("expert")
    n_dp = lax.axis_size("dp")
    n_y = n_dp // 2
    experts, width = router_weight.shape
    exp_dev = experts // n_expert
    per = hidden_act.shape[2]
    slots = exp_dev * per
    ff = hidden_act.shape[3]
    capacity = per // n_expert
    tok_rows, top_count = routes.shape
    shape = jax.ShapeDtypeStruct
    dp_index, expert_index = lax.axis_index("dp"), lax.axis_index("expert")
    y_index = dp_index // 2
    place = jnp.stack([y_index, dp_index % 2, 1 - 2 * (y_index % 2)]).astype(jnp.int32)
    smem = pl.BlockSpec(memory_space=pltpu.SMEM)
    chunk_rows, chunk_wide = n_expert * 8, exp_dev * capacity * width // 8

    chunk, probs, code = call(
        functools.partial(route_kernel, exp_dev, capacity),
        (
            shape((chunk_rows, chunk_wide + LANES), BF16),
            shape((experts, tok_rows), F32),
            shape((experts, tok_rows), F32),
        ),
        2 * tok_rows * experts * width,
        2 * (2 * tok_rows + experts) * width,
        scratch_shapes=[pltpu.VMEM((chunk_wide // LANES + 1, chunk_rows, LANES), F32)],
    )(layer_input, out_grad, router_weight, routes.T)

    chunk = lax.all_to_all(chunk.reshape(n_expert, 8, -1), "expert", split_axis=0, concat_axis=0, tiled=True)
    chunk = chunk.reshape(chunk_rows, -1)

    hidden = hidden_act.reshape(slots, ff)
    y_pairs = exchange_order(n_y)
    groups = len(y_pairs)
    order = [d for pair in reversed(y_pairs) for d in pair]
    def y_swap(odd):
        one_way = [(2 * y + c, (2 * y + 2 + c) % n_dp) for y in range(odd, n_y, 2) for c in range(2)]
        return one_way + [(b, a) for a, b in one_way]

    def add(a, b):
        return (a.astype(F32) + b.astype(F32)).astype(BF16)

    rows, gate, keep, trade = call(
        functools.partial(place_kernel, capacity, [order, [-d for d in order]]),
        (
            shape((slots, width), BF16),
            shape((slots, 1), F32),
            shape((slots, width // 2 + ff), BF16),
            shape((slots, width // 2 + ff), BF16),
        ),
        2 * slots * chunk_rows * LANES,
        2 * slots * (4 * width + 3 * ff),
        in_specs=[smem] + whole(2),
        out_specs=whole(4),
        scratch_shapes=[
            pltpu.VMEM((chunk_wide // LANES // exp_dev, chunk_rows, LANES), F32),
            pltpu.VMEM((width // LANES, per, LANES), F32),
        ],
    )(place, hidden, chunk)

    got = lax.ppermute(trade, "dp", [(i, i ^ 1) for i in range(n_dp)])

    tile = ff // 2 if ff % 256 == 0 else ff
    hidden_grad, back = call(
        functools.partial(product_kernel, capacity),
        (shape((1, exp_dev, per, ff), BF16), shape((n_expert * 8, LANES), BF16)),
        2 * slots * ff * width,
        2 * (slots + exp_dev * ff) * width + 4 * slots * ff,
        grid=(exp_dev, ff // tile),
        in_specs=[
            pl.BlockSpec((per, width), lambda e, f: (e, 0)),
            pl.BlockSpec((per, 1), lambda e, f: (e, 0)),
            pl.BlockSpec((per, tile), lambda e, f: (e, f)),
            pl.BlockSpec((1, tile, width), lambda e, f: (e, f, 0)),
        ],
        out_specs=(
            pl.BlockSpec((1, 1, per, tile), lambda e, f: (0, e, 0, f)),
            pl.BlockSpec((n_expert * 8, LANES), lambda e, f: (0, 0)),
        ),
        scratch_shapes=[pltpu.VMEM((per, 1), F32), pltpu.VMEM((n_expert * 8, LANES), F32)],
    )(rows, gate, hidden, down_weight)

    got, back = lax.optimization_barrier((got, back))
    back = lax.all_to_all(back.reshape(n_expert, 8, LANES), "expert", split_axis=0, concat_axis=0, tiled=True)

    def partials(at, count):
        return call(
            functools.partial(partial_kernel, at, exp_dev),
            [shape((ff, 2 * LANES), BF16)] * (exp_dev * count),
            8 * slots * ff * LANES * count,
            4 * slots * (ff + 2 * LANES * count),
            in_specs=whole(2),
            out_specs=whole(exp_dev * count),
        )(keep, got)

    sums = partials(0, 1)
    later = []
    if groups > 1:
        later = partials(1, groups - 1)
        back = lax.optimization_barrier((back, *later))[0]
    for step in range(groups, 1, -1):
        came = [lax.ppermute(sums[e], "dp", y_swap((step - 1 + e) % 2)) for e in range(exp_dev)]
        mine, later = later[:exp_dev], later[exp_dev:]
        if step > 2:
            sums = [add(a, b) for a, b in zip(mine, came)]
        else:
            away = [add(a[:, LANES:], b[:, LANES:]) for a, b in zip(mine, came)]
            home = [a[:, :LANES].astype(F32) + b[:, :LANES].astype(F32) for a, b in zip(mine, came)]
    if groups == 1:
        away = [a[:, LANES:] for a in sums]
        home = [a[:, :LANES].astype(F32) for a in sums]
    came = [lax.ppermute(away[e], "dp", y_swap(e % 2)) for e in range(exp_dev)]
    down_grad = jnp.stack([a + b.astype(F32) for a, b in zip(home, came)])

    piece = exp_dev * width // 8
    term, input_grad = call(
        functools.partial(router_kernel, capacity, exp_dev),
        (shape((n_expert * 8, piece), BF16), shape((tok_rows, width), BF16)),
        2 * tok_rows * width * (experts + 2 * n_expert * 8),
        2 * (2 * tok_rows + 2 * experts) * width,
    )(back.reshape(n_expert * 8, LANES), probs, code, layer_input, router_weight)

    shares = lax.all_to_all(term.reshape(n_expert, 8, piece), "expert", split_axis=0, concat_axis=0, tiled=True)
    replica_sum = jnp.sum(shares.astype(F32), axis=0)
    copies = jnp.broadcast_to(replica_sum[None], (n_dp, 8, piece))
    gathered = lax.all_to_all(copies, "dp", split_axis=0, concat_axis=0, tiled=True)
    router_grad = jnp.sum(gathered, axis=0).reshape(exp_dev, width)
    return (down_grad, hidden_grad, router_grad, input_grad)


def solution(mesh):
    in_specs = (
        P(("dp", "expert"), None),
        P(("dp", "expert"), None),
        P(),
        P(("dp", "expert"), None),
        P("dp", "expert", None, None),
        P("expert", None, None),
    )
    out_specs = (
        P("expert", None, "dp"),
        P("dp", "expert", None, None),
        P("expert", None),
        P(("dp", "expert"), None),
    )
    return jax.shard_map(
        on_device, mesh=mesh, in_specs=in_specs, out_specs=out_specs, check_vma=False
    )
```

```python
import functools

import jax
import jax.numpy as jnp
from jax import lax
from jax.experimental import pallas as pl
from jax.experimental.pallas import tpu as pltpu
from jax.sharding import PartitionSpec as P

F32 = jnp.float32
BF16 = jnp.bfloat16
LANES = 128
VMEM_BYTES = 18 * 1024 * 1024


def dot(a, b, dims=((1,), (0,))):
    return lax.dot_general(a, b, (dims, ((), ())), preferred_element_type=F32)


def iota(shape, axis):
    return lax.broadcasted_iota(jnp.int32, shape, axis)


def call(body, out_shape, flops, moved, n_smem=0, **kwargs):
    return pl.pallas_call(
        body,
        out_shape=out_shape,
        compiler_params=pltpu.CompilerParams(vmem_limit_bytes=VMEM_BYTES),
        cost_estimate=pl.CostEstimate(flops=flops, bytes_accessed=moved, transcendentals=0),
        **kwargs,
    )


def whole(n):
    return [pl.BlockSpec(memory_space=pltpu.VMEM)] * n


def narrow(tiles, out_ref):
    for k in range(tiles.shape[0]):
        out_ref[:, k * LANES : (k + 1) * LANES] = tiles[k].astype(BF16)


def route_kernel(exp_dev, capacity, x_ref, grad_ref, rw_ref, routes_ref, chunk_ref, probs_ref, code_ref, buffer):
    experts = rw_ref.shape[0]
    top, rows = routes_ref.shape
    ids = iota((experts, rows), 0)
    chosen = ids == routes_ref[0:1, :]
    for k in range(1, top):
        chosen = chosen | (ids == routes_ref[k : k + 1, :])
    logits = dot(rw_ref[...], x_ref[...], ((1,), (1,)))
    highest = jnp.max(jnp.where(chosen, logits, -jnp.inf), axis=0, keepdims=True)
    weights = jnp.where(chosen, jnp.exp(jnp.where(chosen, logits - highest, 0.0)), 0.0)
    probs = weights / jnp.sum(weights, axis=0, keepdims=True)
    earlier = jnp.where(iota((rows, rows), 0) < iota((rows, rows), 1), 1.0, 0.0).astype(BF16)
    position = dot(jnp.where(chosen, 1.0, 0.0).astype(BF16), earlier)
    code = jnp.where(chosen, position, -1.0)
    probs_ref[...] = probs
    code_ref[...] = code
    n_dev = experts // exp_dev
    lane = iota((n_dev, LANES), 1)
    gates = jnp.zeros((n_dev, LANES), F32)
    piece = grad_ref.shape[1] // 8
    tiles = piece // LANES
    for e in range(exp_dev):
        owner = jnp.where(iota((n_dev, experts), 1) == iota((n_dev, experts), 0) * exp_dev + e, 1.0, 0.0).astype(BF16)
        own = dot(owner, code.astype(BF16))
        own_probs = dot(owner, probs.astype(BF16))
        select = [jnp.where(own == c, 1.0, 0.0) for c in range(capacity)]
        picked = dot(jnp.concatenate(select, axis=0).astype(BF16), grad_ref[...])
        for c in range(capacity):
            gate = jnp.sum(select[c] * own_probs, axis=1, keepdims=True)
            gates = jnp.where(lane == e * capacity + c, gate, gates)
            for p in range(8):
                for j in range(tiles):
                    column = p * piece + j * LANES
                    buffer.at[(e * capacity + c) * tiles + j][pl.ds(p, n_dev, stride=8), :] = picked[
                        c * n_dev : (c + 1) * n_dev, column : column + LANES
                    ]
    for p in range(8):
        buffer.at[buffer.shape[0] - 1][pl.ds(p, n_dev, stride=8), :] = gates
    narrow(buffer, chunk_ref)


def place_kernel(capacity, order, place_ref, hidden_ref, chunk_ref, rows_ref, gate_ref, keep_ref, trade_ref, buffer, wide):
    slots, width = rows_ref.shape
    exp_dev = len(order)
    per = slots // exp_dev
    n_source = per // capacity
    piece, half = width // 8, width // 2
    tiles = piece // LANES
    spread = jnp.where(
        iota((per, n_source * 8), 1) == lax.div(iota((per, n_source * 8), 0), capacity) * 8, 1.0, 0.0
    ).astype(BF16)
    gates = dot(spread, chunk_ref[:, chunk_ref.shape[1] - LANES :])
    n_y = len(order[0])
    for e in range(exp_dev):
        span = slice(e * per, (e + 1) * per)
        for k in range(capacity * tiles):
            at = e * capacity * tiles + k
            buffer[k] = chunk_ref[:, at * LANES : (at + 1) * LANES].astype(F32)
        for c in range(capacity):
            for p in range(8):
                for j in range(tiles):
                    wide.at[p * tiles + j][pl.ds(c, n_source, stride=capacity), :] = buffer.at[c * tiles + j][
                        pl.ds(p, n_source, stride=8), :
                    ]
        for k in range(width // LANES):
            rows_ref[span, k * LANES : (k + 1) * LANES] = wide[k].astype(BF16)
        lane = e * capacity + lax.rem(iota((per, LANES), 0), capacity)
        gate = jnp.sum(jnp.where(iota((per, LANES), 1) == lane, gates, 0.0), axis=1, keepdims=True)
        gate_ref[span, :] = gate
        gated = (gate * hidden_ref[span, :].astype(F32)).astype(BF16)
        keep_ref[span, half:] = gated
        trade_ref[span, half:] = gated
        for k, delta in enumerate(order[e]):
            chip = lax.rem(place_ref[0] + place_ref[2] * delta + n_y, n_y)
            mine = pl.multiple_of((2 * chip + place_ref[1]) * LANES, LANES)
            other = pl.multiple_of((2 * chip + 1 - place_ref[1]) * LANES, LANES)
            column = slice(k * LANES, (k + 1) * LANES)
            keep_ref[span, column] = rows_ref[span, pl.ds(mine, LANES)]
            trade_ref[span, column] = rows_ref[span, pl.ds(other, LANES)]


def product_kernel(capacity, rows_ref, gate_ref, hidden_ref, weight_ref, grad_ref, back_ref):
    exp_dev = weight_ref.shape[0]
    slots = rows_ref.shape[0] // exp_dev
    lane = iota((slots, LANES), 1)
    place = lax.rem(iota((slots, LANES), 0), capacity)
    row = iota((back_ref.shape[0], slots), 0)
    source = lax.div(iota((back_ref.shape[0], slots), 1), capacity) * 8
    total = jnp.zeros(back_ref.shape, F32)
    for e in range(exp_dev):
        span = slice(e * slots, (e + 1) * slots)
        product = dot(rows_ref[span, :], weight_ref[e], ((1,), (1,)))
        grad_ref[0, e] = (gate_ref[span, :] * product).astype(BF16)
        sums = jnp.sum(product * hidden_ref[span, :].astype(F32), axis=1, keepdims=True)
        spread = jnp.where(lane == e * capacity + place, sums, 0.0)
        high = spread.astype(BF16)
        rest = spread - high.astype(F32)
        middle = rest.astype(BF16)
        low = (rest - middle.astype(F32)).astype(BF16)
        for i, piece in enumerate((high, middle, low)):
            total += dot(jnp.where(row == source + i, 1.0, 0.0).astype(BF16), piece)
    back_ref[...] = total.astype(BF16)


def partial_kernel(first, exp_dev, mine_ref, got_ref, *outs):
    ff, wide = outs[0].shape
    half = mine_ref.shape[1] - ff
    per = mine_ref.shape[0] // exp_dev
    groups = len(outs) // exp_dev
    for e in range(exp_dev):
        span = slice(e * per, (e + 1) * per)
        mine, got = mine_ref[span, half:], got_ref[span, half:]
        for g in range(groups):
            column = slice((first + g) * wide, (first + g + 1) * wide)
            total = dot(mine, mine_ref[span, column], ((0,), (0,)))
            total += dot(got, got_ref[span, column], ((0,), (0,)))
            outs[g * exp_dev + e][...] = total.astype(BF16)


def router_kernel(capacity, exp_dev, back_ref, probs_ref, code_ref, x_ref, rw_ref, term_ref, grad_ref):
    experts, rows = probs_ref.shape
    parts = back_ref.shape[0]
    width = rw_ref.shape[1]
    ids = lax.div(iota((experts, parts), 0), exp_dev)
    column = iota((experts, parts), 1)
    owner = jnp.where((lax.div(column, 8) == ids) & (lax.rem(column, 8) < 3), 1.0, 0.0).astype(BF16)
    spread = dot(owner, back_ref[...])
    lane = iota((experts, LANES), 1)
    start = lax.rem(iota((experts, LANES), 0), exp_dev) * capacity
    code = code_ref[...]
    probs = probs_ref[...]
    gate_grad = jnp.zeros((experts, rows), F32)
    for c in range(capacity):
        column = jnp.sum(jnp.where(lane == start + c, spread, 0.0), axis=1, keepdims=True)
        gate_grad += jnp.where(code == c, column, 0.0)
    weighted = jnp.sum(probs * gate_grad, axis=0, keepdims=True)
    logit_grad = probs * (gate_grad - weighted)
    high = logit_grad.astype(BF16)
    low = (logit_grad - high.astype(F32)).astype(BF16)
    grad_ref[...] = dot(high, rw_ref[...], ((0,), (0,))).astype(BF16)
    out_rows, piece = term_ref.shape
    split = width // piece
    row = iota((out_rows, experts), 0)
    first = iota((out_rows, experts), 1) * split
    repeat = jnp.where((row >= first) & (row < first + split), 1.0, 0.0).astype(BF16)
    high = dot(repeat, high).astype(BF16)
    low = dot(repeat, low).astype(BF16)
    quarter = lax.rem(iota((out_rows, 1), 0), split)
    total = jnp.zeros((out_rows, piece), F32)
    for q in range(split):
        x = x_ref[:, q * piece : (q + 1) * piece]
        total += jnp.where(quarter == q, dot(high, x) + dot(low, x), 0.0)
    term_ref[...] = total.astype(BF16)


def exchange_order(n):
    pairs = [[0, 1]]
    for step in range(1, n // 2):
        pairs.append([-step, -step - 1] if step % 2 else [step, step + 1])
    return pairs


def on_device(layer_input, out_grad, router_weight, routes, hidden_act, down_weight):
    n_expert = lax.axis_size("expert")
    n_dp = lax.axis_size("dp")
    n_y = n_dp // 2
    experts, width = router_weight.shape
    exp_dev = experts // n_expert
    per = hidden_act.shape[2]
    slots = exp_dev * per
    ff = hidden_act.shape[3]
    capacity = per // n_expert
    tok_rows, top_count = routes.shape
    shape = jax.ShapeDtypeStruct
    dp_index, expert_index = lax.axis_index("dp"), lax.axis_index("expert")
    y_index = dp_index // 2
    place = jnp.stack([y_index, dp_index % 2, 1 - 2 * (y_index % 2)]).astype(jnp.int32)
    smem = pl.BlockSpec(memory_space=pltpu.SMEM)
    chunk_rows, chunk_wide = n_expert * 8, exp_dev * capacity * width // 8

    chunk, probs, code = call(
        functools.partial(route_kernel, exp_dev, capacity),
        (
            shape((chunk_rows, chunk_wide + LANES), BF16),
            shape((experts, tok_rows), F32),
            shape((experts, tok_rows), F32),
        ),
        2 * tok_rows * experts * width,
        2 * (2 * tok_rows + experts) * width,
        scratch_shapes=[pltpu.VMEM((chunk_wide // LANES + 1, chunk_rows, LANES), F32)],
    )(layer_input, out_grad, router_weight, routes.T)

    chunk = lax.all_to_all(chunk.reshape(n_expert, 8, -1), "expert", split_axis=0, concat_axis=0, tiled=True)
    chunk = chunk.reshape(chunk_rows, -1)

    hidden = hidden_act.reshape(slots, ff)
    y_pairs = exchange_order(n_y)
    groups = len(y_pairs)
    order = [d for pair in reversed(y_pairs) for d in pair]
    def y_swap(odd):
        one_way = [(2 * y + c, (2 * y + 2 + c) % n_dp) for y in range(odd, n_y, 2) for c in range(2)]
        return one_way + [(b, a) for a, b in one_way]

    def add(a, b):
        return (a.astype(F32) + b.astype(F32)).astype(BF16)

    rows, gate, keep, trade = call(
        functools.partial(place_kernel, capacity, [order, [-d for d in order]]),
        (
            shape((slots, width), BF16),
            shape((slots, 1), F32),
            shape((slots, width // 2 + ff), BF16),
            shape((slots, width // 2 + ff), BF16),
        ),
        2 * slots * chunk_rows * LANES,
        2 * slots * (4 * width + 3 * ff),
        in_specs=[smem] + whole(2),
        out_specs=whole(4),
        scratch_shapes=[
            pltpu.VMEM((chunk_wide // LANES // exp_dev, chunk_rows, LANES), F32),
            pltpu.VMEM((width // LANES, per, LANES), F32),
        ],
    )(place, hidden, chunk)

    hidden_grad, back = call(
        functools.partial(product_kernel, capacity),
        (shape((1, exp_dev, per, ff), BF16), shape((chunk_rows, LANES), BF16)),
        2 * slots * ff * width,
        2 * (slots + exp_dev * ff) * width + 4 * slots * ff,
        in_specs=whole(4),
        out_specs=whole(2),
    )(rows, gate, hidden, down_weight)

    trade, back = lax.optimization_barrier((trade, back))
    got = lax.ppermute(trade, "dp", [(i, i ^ 1) for i in range(n_dp)])

    back = lax.all_to_all(back.reshape(n_expert, 8, LANES), "expert", split_axis=0, concat_axis=0, tiled=True)

    def partials(at, count):
        return call(
            functools.partial(partial_kernel, at, exp_dev),
            [shape((ff, 2 * LANES), BF16)] * (exp_dev * count),
            8 * slots * ff * LANES * count,
            4 * slots * (ff + 2 * LANES * count),
            in_specs=whole(2),
            out_specs=whole(exp_dev * count),
        )(keep, got)

    sums = partials(0, 1)
    later = []
    if groups > 1:
        later = partials(1, groups - 1)
        back = lax.optimization_barrier((back, *later))[0]
    piece = exp_dev * width // 8
    term, input_grad = call(
        functools.partial(router_kernel, capacity, exp_dev),
        (shape((n_expert * 8, piece), BF16), shape((tok_rows, width), BF16)),
        2 * tok_rows * width * (experts + 2 * n_expert * 8),
        2 * (2 * tok_rows + 2 * experts) * width,
    )(back.reshape(n_expert * 8, LANES), probs, code, layer_input, router_weight)

    shares = lax.all_to_all(term.reshape(n_expert, 8, piece), "expert", split_axis=0, concat_axis=0, tiled=True)
    replica_sum = jnp.sum(shares.astype(F32), axis=0)
    copies = jnp.broadcast_to(replica_sum[None], (n_dp, 8, piece))
    for step in range(groups, 1, -1):
        came = [lax.ppermute(sums[e], "dp", y_swap((step - 1 + e) % 2)) for e in range(exp_dev)]
        mine, later = later[:exp_dev], later[exp_dev:]
        if step == 2:
            copies, *came = lax.optimization_barrier((copies, *came))
        if step > 2:
            sums = [add(a, b) for a, b in zip(mine, came)]
        else:
            away = [add(a[:, LANES:], b[:, LANES:]) for a, b in zip(mine, came)]
            home = [a[:, :LANES].astype(F32) + b[:, :LANES].astype(F32) for a, b in zip(mine, came)]
    if groups == 1:
        away = [a[:, LANES:] for a in sums]
        home = [a[:, :LANES].astype(F32) for a in sums]
    came = [lax.ppermute(away[e], "dp", y_swap(e % 2)) for e in range(exp_dev)]
    down_grad = jnp.stack([a + b.astype(F32) for a, b in zip(home, came)])

    gathered = lax.all_to_all(copies, "dp", split_axis=0, concat_axis=0, tiled=True)
    router_grad = jnp.sum(gathered, axis=0).reshape(exp_dev, width)
    return (down_grad, hidden_grad, router_grad, input_grad)


def solution(mesh):
    in_specs = (
        P(("dp", "expert"), None),
        P(("dp", "expert"), None),
        P(),
        P(("dp", "expert"), None),
        P("dp", "expert", None, None),
        P("expert", None, None),
    )
    out_specs = (
        P("expert", None, "dp"),
        P("dp", "expert", None, None),
        P("expert", None),
        P(("dp", "expert"), None),
    )
    return jax.shard_map(
        on_device, mesh=mesh, in_specs=in_specs, out_specs=out_specs, check_vma=False
    )
```

```python
import functools

import jax
import jax.numpy as jnp
from jax import lax
from jax.experimental import pallas as pl
from jax.experimental.pallas import tpu as pltpu
from jax.sharding import PartitionSpec as P

F32 = jnp.float32
BF16 = jnp.bfloat16
LANES = 128
VMEM_BYTES = 28 * 1024 * 1024


def dot(a, b, dims=((1,), (0,))):
    return lax.dot_general(a, b, (dims, ((), ())), preferred_element_type=F32)


def iota(shape, axis):
    return lax.broadcasted_iota(jnp.int32, shape, axis)


def call(body, out_shape, flops, moved, n_smem=0, **kwargs):
    return pl.pallas_call(
        body,
        out_shape=out_shape,
        compiler_params=pltpu.CompilerParams(vmem_limit_bytes=VMEM_BYTES),
        cost_estimate=pl.CostEstimate(flops=flops, bytes_accessed=moved, transcendentals=0),
        **kwargs,
    )


def whole(n):
    return [pl.BlockSpec(memory_space=pltpu.VMEM)] * n


def narrow(tiles, out_ref):
    for k in range(tiles.shape[0]):
        out_ref[:, k * LANES : (k + 1) * LANES] = tiles[k].astype(BF16)


def route_kernel(exp_dev, capacity, x_ref, grad_ref, rw_ref, routes_ref, chunk_ref, probs_ref, code_ref, buffer):
    experts = rw_ref.shape[0]
    top, rows = routes_ref.shape
    ids = iota((experts, rows), 0)
    chosen = ids == routes_ref[0:1, :]
    for k in range(1, top):
        chosen = chosen | (ids == routes_ref[k : k + 1, :])
    logits = dot(rw_ref[...], x_ref[...], ((1,), (1,)))
    highest = jnp.max(jnp.where(chosen, logits, -jnp.inf), axis=0, keepdims=True)
    weights = jnp.where(chosen, jnp.exp(jnp.where(chosen, logits - highest, 0.0)), 0.0)
    probs = weights / jnp.sum(weights, axis=0, keepdims=True)
    earlier = jnp.where(iota((rows, rows), 0) < iota((rows, rows), 1), 1.0, 0.0).astype(BF16)
    position = dot(jnp.where(chosen, 1.0, 0.0).astype(BF16), earlier)
    code = jnp.where(chosen, position, -1.0)
    probs_ref[...] = probs
    code_ref[...] = code
    n_dev = experts // exp_dev
    lane = iota((n_dev, LANES), 1)
    gates = jnp.zeros((n_dev, LANES), F32)
    piece = grad_ref.shape[1] // 8
    tiles = piece // LANES
    for e in range(exp_dev):
        owner = jnp.where(iota((n_dev, experts), 1) == iota((n_dev, experts), 0) * exp_dev + e, 1.0, 0.0).astype(BF16)
        own = dot(owner, code.astype(BF16))
        own_probs = dot(owner, probs.astype(BF16))
        select = [jnp.where(own == c, 1.0, 0.0) for c in range(capacity)]
        picked = dot(jnp.concatenate(select, axis=0).astype(BF16), grad_ref[...])
        for c in range(capacity):
            gate = jnp.sum(select[c] * own_probs, axis=1, keepdims=True)
            gates = jnp.where(lane == e * capacity + c, gate, gates)
            for p in range(8):
                for j in range(tiles):
                    column = p * piece + j * LANES
                    buffer.at[(e * capacity + c) * tiles + j][pl.ds(p, n_dev, stride=8), :] = picked[
                        c * n_dev : (c + 1) * n_dev, column : column + LANES
                    ]
    for p in range(8):
        buffer.at[buffer.shape[0] - 1][pl.ds(p, n_dev, stride=8), :] = gates
    narrow(buffer, chunk_ref)


def place_kernel(capacity, exp_dev, hidden_ref, chunk_ref, rows_ref, gate_ref, gated_ref, buffer, wide):
    slots, width = rows_ref.shape
    per = slots // exp_dev
    n_source = per // capacity
    piece = width // 8
    tiles = piece // LANES
    spread = jnp.where(
        iota((per, n_source * 8), 1) == lax.div(iota((per, n_source * 8), 0), capacity) * 8, 1.0, 0.0
    ).astype(BF16)
    gates = dot(spread, chunk_ref[:, chunk_ref.shape[1] - LANES :])
    for e in range(exp_dev):
        span = slice(e * per, (e + 1) * per)
        for k in range(capacity * tiles):
            at = e * capacity * tiles + k
            buffer[k] = chunk_ref[:, at * LANES : (at + 1) * LANES].astype(F32)
        for c in range(capacity):
            for p in range(8):
                for j in range(tiles):
                    wide.at[p * tiles + j][pl.ds(c, n_source, stride=capacity), :] = buffer.at[c * tiles + j][
                        pl.ds(p, n_source, stride=8), :
                    ]
        for k in range(width // LANES):
            rows_ref[span, k * LANES : (k + 1) * LANES] = wide[k].astype(BF16)
        lane = e * capacity + lax.rem(iota((per, LANES), 0), capacity)
        gate = jnp.sum(jnp.where(iota((per, LANES), 1) == lane, gates, 0.0), axis=1, keepdims=True)
        gate_ref[span, :] = gate
        gated_ref[span, :] = (gate * hidden_ref[span, :].astype(F32)).astype(BF16)


def product_kernel(capacity, rows_ref, gate_ref, hidden_ref, weight_ref, grad_ref, back_ref, sums, total):
    e, f = pl.program_id(0), pl.program_id(1)
    slots = rows_ref.shape[0]
    product = dot(rows_ref[...], weight_ref[0], ((1,), (1,)))
    grad_ref[0, 0] = (gate_ref[...] * product).astype(BF16)
    part = jnp.sum(product * hidden_ref[...].astype(F32), axis=1, keepdims=True)

    @pl.when(f == 0)
    def _():
        sums[...] = part

    @pl.when(f > 0)
    def _():
        sums[...] += part

    @pl.when((e == 0) & (f == 0))
    def _():
        total[...] = jnp.zeros_like(total)

    @pl.when(f == pl.num_programs(1) - 1)
    def _():
        lane = iota((slots, LANES), 1)
        slot = iota((slots, LANES), 0)
        spread = jnp.where(lane == e * capacity + lax.rem(slot, capacity), sums[...], 0.0)
        row = iota((total.shape[0], slots), 0)
        source = lax.div(iota((total.shape[0], slots), 1), capacity)
        high = spread.astype(BF16)
        rest = spread - high.astype(F32)
        middle = rest.astype(BF16)
        low = (rest - middle.astype(F32)).astype(BF16)
        for i, piece in enumerate((high, middle, low)):
            group = jnp.where(row == source * 8 + i, 1.0, 0.0).astype(BF16)
            total[...] += dot(group, piece)

    @pl.when((e == pl.num_programs(0) - 1) & (f == pl.num_programs(1) - 1))
    def _():
        back_ref[...] = total[...].astype(BF16)


def partial_kernel(exp_dev, gated_ref, rows_ref, out_ref):
    ff = gated_ref.shape[1]
    per = gated_ref.shape[0] // exp_dev
    for e in range(exp_dev):
        span = slice(e * per, (e + 1) * per)
        total = dot(gated_ref[span, :], rows_ref[span, :], ((0,), (0,))).astype(BF16)
        for i in range(out_ref.shape[0]):
            out_ref[i, e * ff : (e + 1) * ff, :] = total[:, i * LANES : (i + 1) * LANES]


def router_kernel(capacity, exp_dev, back_ref, probs_ref, code_ref, x_ref, rw_ref, term_ref, grad_ref):
    experts, rows = probs_ref.shape
    parts = back_ref.shape[0]
    width = rw_ref.shape[1]
    ids = lax.div(iota((experts, parts), 0), exp_dev)
    column = iota((experts, parts), 1)
    owner = jnp.where((lax.div(column, 8) == ids) & (lax.rem(column, 8) < 3), 1.0, 0.0).astype(BF16)
    spread = dot(owner, back_ref[...])
    lane = iota((experts, LANES), 1)
    start = lax.rem(iota((experts, LANES), 0), exp_dev) * capacity
    code = code_ref[...]
    probs = probs_ref[...]
    gate_grad = jnp.zeros((experts, rows), F32)
    for c in range(capacity):
        column = jnp.sum(jnp.where(lane == start + c, spread, 0.0), axis=1, keepdims=True)
        gate_grad += jnp.where(code == c, column, 0.0)
    weighted = jnp.sum(probs * gate_grad, axis=0, keepdims=True)
    logit_grad = probs * (gate_grad - weighted)
    high = logit_grad.astype(BF16)
    low = (logit_grad - high.astype(F32)).astype(BF16)
    grad_ref[...] = dot(high, rw_ref[...], ((0,), (0,))).astype(BF16)
    out_rows, piece = term_ref.shape
    split = width // piece
    row = iota((out_rows, experts), 0)
    first = iota((out_rows, experts), 1) * split
    repeat = jnp.where((row >= first) & (row < first + split), 1.0, 0.0).astype(BF16)
    high = dot(repeat, high).astype(BF16)
    low = dot(repeat, low).astype(BF16)
    quarter = lax.rem(iota((out_rows, 1), 0), split)
    total = jnp.zeros((out_rows, piece), F32)
    for q in range(split):
        x = x_ref[:, q * piece : (q + 1) * piece]
        total += jnp.where(quarter == q, dot(high, x) + dot(low, x), 0.0)
    term_ref[...] = total.astype(BF16)


def on_device(layer_input, out_grad, router_weight, routes, hidden_act, down_weight):
    n_expert = lax.axis_size("expert")
    n_dp = lax.axis_size("dp")
    experts, width = router_weight.shape
    exp_dev = experts // n_expert
    per = hidden_act.shape[2]
    slots = exp_dev * per
    ff = hidden_act.shape[3]
    capacity = per // n_expert
    tok_rows, top_count = routes.shape
    shape = jax.ShapeDtypeStruct
    chunk_rows, chunk_wide = n_expert * 8, exp_dev * capacity * width // 8

    chunk, probs, code = call(
        functools.partial(route_kernel, exp_dev, capacity),
        (
            shape((chunk_rows, chunk_wide + LANES), BF16),
            shape((experts, tok_rows), F32),
            shape((experts, tok_rows), F32),
        ),
        2 * tok_rows * experts * width,
        2 * (2 * tok_rows + experts) * width,
        scratch_shapes=[pltpu.VMEM((chunk_wide // LANES + 1, chunk_rows, LANES), F32)],
    )(layer_input, out_grad, router_weight, routes.T)

    chunk = lax.all_to_all(chunk.reshape(n_expert, 8, -1), "expert", split_axis=0, concat_axis=0, tiled=True)
    chunk = chunk.reshape(chunk_rows, -1)

    hidden = hidden_act.reshape(slots, ff)
    rows, gate, gated = call(
        functools.partial(place_kernel, capacity, exp_dev),
        (shape((slots, width), BF16), shape((slots, 1), F32), shape((slots, ff), BF16)),
        2 * slots * chunk_rows * LANES,
        2 * slots * (4 * width + 2 * ff),
        in_specs=whole(2),
        out_specs=whole(3),
        scratch_shapes=[
            pltpu.VMEM((chunk_wide // LANES // exp_dev, chunk_rows, LANES), F32),
            pltpu.VMEM((width // LANES, per, LANES), F32),
        ],
    )(hidden, chunk)

    partial_grad = call(
        functools.partial(partial_kernel, exp_dev),
        shape((n_dp, exp_dev * ff, LANES), BF16),
        2 * slots * ff * width,
        2 * (slots * (ff + width) + exp_dev * ff * width),
        grid=(n_dp // 2,),
        in_specs=[
            pl.BlockSpec((slots, ff), lambda k: (0, 0)),
            pl.BlockSpec((slots, 2 * LANES), lambda k: (0, k)),
        ],
        out_specs=pl.BlockSpec((2, exp_dev * ff, LANES), lambda k: (k, 0, 0)),
    )(gated, rows)
    rows, partial_grad = lax.optimization_barrier((rows, partial_grad))
    down_grad = lax.psum_scatter(partial_grad, "dp", scatter_dimension=0, tiled=True)
    down_grad = down_grad.astype(F32).reshape(exp_dev, ff, LANES)

    tile = ff // 2 if ff % 256 == 0 else ff
    hidden_grad, back = call(
        functools.partial(product_kernel, capacity),
        (shape((1, exp_dev, per, ff), BF16), shape((n_expert * 8, LANES), BF16)),
        2 * slots * ff * width,
        2 * (slots + exp_dev * ff) * width + 4 * slots * ff,
        grid=(exp_dev, ff // tile),
        in_specs=[
            pl.BlockSpec((per, width), lambda e, f: (e, 0)),
            pl.BlockSpec((per, 1), lambda e, f: (e, 0)),
            pl.BlockSpec((per, tile), lambda e, f: (e, f)),
            pl.BlockSpec((1, tile, width), lambda e, f: (e, f, 0)),
        ],
        out_specs=(
            pl.BlockSpec((1, 1, per, tile), lambda e, f: (0, e, 0, f)),
            pl.BlockSpec((n_expert * 8, LANES), lambda e, f: (0, 0)),
        ),
        scratch_shapes=[pltpu.VMEM((per, 1), F32), pltpu.VMEM((n_expert * 8, LANES), F32)],
    )(rows, gate, hidden, down_weight)

    back = lax.all_to_all(back.reshape(n_expert, 8, LANES), "expert", split_axis=0, concat_axis=0, tiled=True)

    piece = exp_dev * width // 8
    term, input_grad = call(
        functools.partial(router_kernel, capacity, exp_dev),
        (shape((n_expert * 8, piece), BF16), shape((tok_rows, width), BF16)),
        2 * tok_rows * width * (experts + 2 * n_expert * 8),
        2 * (2 * tok_rows + 2 * experts) * width,
    )(back.reshape(n_expert * 8, LANES), probs, code, layer_input, router_weight)

    shares = lax.all_to_all(term.reshape(n_expert, 8, piece), "expert", split_axis=0, concat_axis=0, tiled=True)
    replica_sum = jnp.sum(shares.astype(F32), axis=0)
    copies = jnp.broadcast_to(replica_sum[None], (n_dp, 8, piece))
    gathered = lax.all_to_all(copies, "dp", split_axis=0, concat_axis=0, tiled=True)
    router_grad = jnp.sum(gathered, axis=0).reshape(exp_dev, width)
    return (down_grad, hidden_grad, router_grad, input_grad)


def solution(mesh):
    in_specs = (
        P(("dp", "expert"), None),
        P(("dp", "expert"), None),
        P(),
        P(("dp", "expert"), None),
        P("dp", "expert", None, None),
        P("expert", None, None),
    )
    out_specs = (
        P("expert", None, "dp"),
        P("dp", "expert", None, None),
        P("expert", None),
        P(("dp", "expert"), None),
    )
    return jax.shard_map(
        on_device, mesh=mesh, in_specs=in_specs, out_specs=out_specs, check_vma=False
    )
```
